32 devices in a mesh: seq: 2 (over x), chan: 16 (over z, y, core).
Axes of the slice: x: 2, y: 2, z: 4, core: 2. Of those that a mesh axis runs over, the one named last changes fastest.
Arguments:
- activations: bfloat16 [1024, 4096], P('seq', 'chan'), may hold values from -6 to 6
- in_weight: bfloat16 [3, 4096, 4096], P(None, 'chan'), may hold values from -0.09375 to 0.09375
- short_taps: float32 [3, 3, 4096], P(None, None, 'chan'), may hold values from -3.5 to 3.5
- long_filter: bfloat16 [4096, 1024], P('chan', 'seq'), may hold values from -0.1875 to 0.1875
- skip_gain: float32 [4096], P('chan'), may hold values from -4 to 4
Outputs:
- mixed: bfloat16 [1024, 4096], P('seq', 'chan')
The draws below stay inside these ranges and needn't reach their ends.
All inputs are finite; a program needn't handle non-finite values.
Results may differ from the reference program's by a relative error of at most 0.0076.
Values may be sent and summed in bfloat16 or wider, within the bound.
A program may use at most 64 MiB of HBM per device.

```python
import math
import jax
import jax.numpy as jnp
from jax import lax

D = 4096
TOK_DEV = 512
TOKENS = 1024


def levels(key, dims, pieces, least, largest):
    def one(dim, shards_of):
        heights = jax.random.uniform(jax.random.fold_in(jax.random.fold_in(key, 6), dim), (shards_of,), jnp.float32, least / len(pieces), largest / len(pieces))
        return jnp.repeat(jnp.exp(heights), dims[dim] // shards_of).reshape((-1,) + (1,) * (len(dims) - dim - 1))

    loudness = one(*pieces[0])
    for cut in pieces[1:]:
        loudness = loudness * one(*cut)
    return loudness


def normal_values(key, extent, scale, most, pieces=(), held_as=jnp.bfloat16):
    values = scale * jax.random.normal(key, extent, jnp.float32)
    if pieces:
        values = values * levels(key, extent, pieces, -0.22, 0.18)
    return jnp.clip(values, -most, most).astype(held_as)


def setup_inputs(seed: int = 0) -> dict:
    seeds = jax.random.split(jax.random.key(seed), 6)
    activations = normal_values(seeds[0], (TOKENS, D), 1.0, 6.0, ((0, 2), (1, 16)))
    in_weight = normal_values(seeds[1], (3, D, D), D ** -0.5, 0.09375, ((1, 16),))
    short_taps = normal_values(seeds[2], (3, 3, D), 3 ** -0.5, 3.5, ((2, 16),), jnp.float32)
    long_filter = normal_values(seeds[3], (D, TOKENS), TOKENS ** -0.5, 0.1875, ((0, 16), (1, 2)))
    skip_gain = normal_values(seeds[4], (D,), 1.0, 4.0, ((0, 16),), jnp.float32)
    return {"activations": activations, "in_weight": in_weight, "short_taps": short_taps, "long_filter": long_filter, "skip_gain": skip_gain}


def tables(length):
    double = 2 * length
    freq_index = jnp.arange(double, dtype=jnp.int32)
    phase = ((freq_index[:, None] * freq_index[None, :]) % double).astype(jnp.float32) * (2.0 * math.pi / double)
    return jnp.cos(phase).astype(jnp.bfloat16), jnp.sin(phase).astype(jnp.bfloat16)


def reference(activations, in_weight, short_taps, long_filter, skip_gain):
    length = activations.shape[0]
    width = activations.shape[1]
    flat_weight = in_weight.reshape(3 * width, width)
    proj = jnp.dot(activations, flat_weight.T, preferred_element_type=jnp.float32).astype(jnp.bfloat16)
    proj = proj.reshape(length, 3, width).astype(jnp.float32)
    padded = jnp.concatenate([jnp.zeros((2, 3, width), jnp.float32), proj], axis=0)
    feat = short_taps[:, 0, :] * padded[2:] + short_taps[:, 1, :] * padded[1:-1] + short_taps[:, 2, :] * padded[:-2]
    gated = (feat[:, 1, :] * feat[:, 2, :]).astype(jnp.bfloat16)
    block = TOK_DEV
    count = length // block
    double = 2 * block
    cos_table, sin_table = tables(block)
    cos_fwd = cos_table[:, :block].astype(jnp.float32)
    sin_fwd = sin_table[:, :block].astype(jnp.float32)
    highest = lax.Precision.HIGHEST
    sig_blocks = gated.astype(jnp.float32).reshape(count, block, width)
    sig_re = jnp.einsum("ft,btc->bfc", cos_fwd, sig_blocks, precision=highest)
    sig_im = -jnp.einsum("ft,btc->bfc", sin_fwd, sig_blocks, precision=highest)
    fil_blocks = long_filter.astype(jnp.float32).reshape(width, count, block)
    fil_re = jnp.einsum("ft,cbt->bfc", cos_fwd, fil_blocks, precision=highest)
    fil_im = -jnp.einsum("ft,cbt->bfc", sin_fwd, fil_blocks, precision=highest)
    cos_inv = cos_table.astype(jnp.float32)
    sin_inv = sin_table.astype(jnp.float32)
    outputs = []
    for index in range(count):
        cur_re = jnp.zeros((double, width), jnp.float32)
        cur_im = jnp.zeros((double, width), jnp.float32)
        prev_re = jnp.zeros((double, width), jnp.float32)
        prev_im = jnp.zeros((double, width), jnp.float32)
        for source in range(index + 1):
            lag = index - source
            cur_re = cur_re + fil_re[lag] * sig_re[source] - fil_im[lag] * sig_im[source]
            cur_im = cur_im + fil_re[lag] * sig_im[source] + fil_im[lag] * sig_re[source]
            if lag >= 1:
                prev_re = prev_re + fil_re[lag - 1] * sig_re[source] - fil_im[lag - 1] * sig_im[source]
                prev_im = prev_im + fil_re[lag - 1] * sig_im[source] + fil_im[lag - 1] * sig_re[source]
        cur_re = cur_re.astype(jnp.bfloat16).astype(jnp.float32)
        cur_im = cur_im.astype(jnp.bfloat16).astype(jnp.float32)
        prev_re = prev_re.astype(jnp.bfloat16).astype(jnp.float32)
        prev_im = prev_im.astype(jnp.bfloat16).astype(jnp.float32)
        part = (jnp.dot(cos_inv[:block], cur_re, precision=highest)
                - jnp.dot(sin_inv[:block], cur_im, precision=highest)
                + jnp.dot(cos_inv[block:], prev_re, precision=highest)
                - jnp.dot(sin_inv[block:], prev_im, precision=highest)) / double
        outputs.append(part)
    conv = jnp.concatenate(outputs, axis=0)
    return (feat[:, 0, :] * (conv + skip_gain * gated.astype(jnp.float32))).astype(jnp.bfloat16)
```

```python
import functools
import math

import jax
import jax.numpy as jnp
import ml_dtypes
import numpy as np
from jax import lax
from jax.experimental import pallas as pl
from jax.experimental.pallas import tpu as pltpu
from jax.sharding import PartitionSpec as P

MESH = pl.DeviceIdType.MESH
F32 = jnp.float32
BF16 = jnp.bfloat16
CHUNKS = 4
HALO = 8


def from_behind(block, axis, distance):
    devices = range(lax.axis_size(axis))
    route = [(i - distance, i) for i in devices if i - distance in devices]
    return lax.ppermute(block, axis, route)


def half_tables(length):
    double = 2 * length
    index = np.arange(length, dtype=np.int64)
    phase = ((index[:, None] * index[None, :]) % double).astype(np.float32) * np.float32(
        2.0 * math.pi / double
    )
    cosine = np.cos(phase)
    sine = -np.sin(phase)
    sine[0] = 1.0 - 2.0 * (index % 2)
    forward = np.concatenate([cosine, sine], axis=0).astype(ml_dtypes.bfloat16)
    inverse = np.concatenate([cosine, sine.T], axis=1).astype(ml_dtypes.bfloat16)
    return forward, inverse


def times(fil_real, fil_imag, sig_real, sig_imag, first):
    cross = jnp.where(first, 0.0, fil_imag)
    real_part = fil_real * sig_real - cross * sig_imag
    imag_part = jnp.where(first, fil_imag, fil_real) * sig_imag + cross * sig_real
    return real_part, imag_part


def nt_dot(a, b):
    return lax.dot_general(a, b, (((1,), (1,)), ((), ())), preferred_element_type=F32)


def fused_kernel(
    chips, act, weight, taps, filt, gain, fwd_in, inv_in, out,
    blocks, wv, acc, proj, gated, gated_in, lags, fwd, inv, spec, total,
    ring_send, ring_recv, core_send, core_recv, own_sem, weight_sem, load_sem,
    seq_send, seq_recv,
):
    rows, depth = act.shape
    width = taps.shape[-1]
    size = rows // CHUNKS
    far = chips // 2
    full = far - 1
    last_slot = 2 * full + 1

    seq = lax.axis_index("seq")
    chan = lax.axis_index("chan")
    chip, core = chan // 2, chan % 2

    def chip_at(place):
        place = lax.rem(place + 2 * chips, chips)
        return jnp.where(place < far, 2 * place, 2 * (chips - 1 - place) + 1)

    place = jnp.where(chip % 2 == 0, chip // 2, chips - 1 - chip // 2)
    ahead = (chip_at(place + 1) * 2 + core, chip_at(place - 1) * 2 + core)
    sibling = chip * 2 + 1 - core

    def slot_of(d, hop):
        if hop == 0:
            return 0
        return last_slot if hop == far else 1 + d * full + hop - 1

    def slots_at(hop):
        return [slot_of(0, hop)] if hop in (0, far) else [slot_of(0, hop), slot_of(1, hop)]

    def chunk(t):
        return pl.ds(pl.multiple_of(t * size, size), size)

    def ring_copy(d, hop, t):
        src = act.at[chunk(t)] if hop == 1 else blocks.at[0, slot_of(d, hop - 1), t]
        slot = slot_of(d, hop)
        return pltpu.make_async_remote_copy(
            src_ref=src, dst_ref=blocks.at[0, slot, t],
            send_sem=ring_send.at[slot, t], recv_sem=ring_recv.at[slot, t],
            device_id=(seq, ahead[d]), device_id_type=MESH,
        )

    def core_copy(slot, t):
        src = act.at[chunk(t)] if slot == 0 else blocks.at[0, slot, t]
        return pltpu.make_async_remote_copy(
            src_ref=src, dst_ref=blocks.at[1, slot, t],
            send_sem=core_send.at[slot, t], recv_sem=core_recv.at[slot, t],
            device_id=(seq, sibling), device_id_type=MESH,
        )

    def seq_copy(src, dst, n):
        return pltpu.make_async_remote_copy(
            src_ref=src, dst_ref=dst, send_sem=seq_send.at[n], recv_sem=seq_recv.at[n],
            device_id=(1 - seq, chan), device_id_type=MESH,
        )

    def gated_copy(t):
        return seq_copy(gated.at[chunk(t)], gated_in.at[chunk(t)], t)

    def halo_copy():
        return seq_copy(proj.at[:, pl.ds(rows, HALO)], proj.at[:, pl.ds(0, HALO)], CHUNKS)

    def filter_copy():
        return seq_copy(filt, lags.at[0], CHUNKS + 1)

    def own_copy(t):
        return pltpu.make_async_copy(act.at[chunk(t)], blocks.at[0, 0, t], own_sem.at[t])

    def weight_copy(side, slot):
        if slot == 0:
            origin = chip
        elif slot == last_slot:
            origin = chip_at(place + far)
        elif slot <= full:
            origin = chip_at(place - slot)
        else:
            origin = chip_at(place + slot - full)
        block = origin * 2 + (core if side == 0 else 1 - core)
        cols = pl.ds(pl.multiple_of(block * depth, depth), depth)
        return pltpu.make_async_copy(
            weight.at[:, :, cols], wv.at[side, slot], weight_sem.at[side, slot]
        )

    fwd_copy = pltpu.make_async_copy(fwd_in, fwd, load_sem.at[0])
    inv_copy = pltpu.make_async_copy(inv_in, inv, load_sem.at[1])
    lag_copy = pltpu.make_async_copy(filt, lags.at[seq], load_sem.at[2])

    for t in range(CHUNKS):
        own_copy(t).start()
    for slot in range(last_slot + 1):
        for side in range(2):
            weight_copy(side, slot).start()
    lag_copy.start()
    fwd_copy.start()
    inv_copy.start()

    barrier = pltpu.get_barrier_semaphore()
    for target in ((seq, ahead[0]), (seq, ahead[1]), (seq, sibling), (1 - seq, chan)):
        pl.semaphore_signal(barrier, inc=1, device_id=target, device_id_type=MESH)
    pl.semaphore_wait(barrier, 4)

    @pl.when(seq == 0)
    def _():
        proj[:, pl.ds(0, HALO), :] = jnp.zeros((3, HALO, width), F32)

    def short(stream, t):
        window = proj[stream, pl.ds(pl.multiple_of(t * size, size), size + HALO), :]
        return (
            taps[stream, 0, :][None] * window[HALO:]
            + taps[stream, 1, :][None] * window[HALO - 1 : HALO - 1 + size]
            + taps[stream, 2, :][None] * window[HALO - 2 : HALO - 2 + size]
        )

    def gate(t):
        gated[chunk(t), :] = (short(1, t) * short(2, t)).astype(BF16)

    def product(side, hop, t):
        slots = slots_at(hop)

        @pl.when(t == 0)
        def _():
            for slot in slots:
                weight_copy(side, slot).wait()

        x = jnp.concatenate([blocks[side, slot, t] for slot in slots], axis=1)
        w = jnp.concatenate(
            [wv[side, slot].reshape(3 * width, depth) for slot in slots], axis=1
        )
        return nt_dot(x, w)

    hops = list(range(far, -1, -1))

    def step(g, carry):
        for hop in hops:
            t = g - hop

            @pl.when((t >= 0) & (t < CHUNKS))
            def _(hop=hop, t=t):
                if hop == 0:
                    for d in range(2):
                        ring_copy(d, 1, t).start()
                    core_copy(0, t).start()
                elif hop < far:
                    for d in range(2):
                        ring_copy(d, hop, t).wait_recv()
                        if hop < full:
                            ring_copy(d, hop + 1, t).start()
                        else:

                            @pl.when(t % 2 == d)
                            def _(d=d):
                                ring_copy(d, far, t).start()

                        core_copy(slot_of(d, hop), t).start()
                else:
                    ring_copy(0, far, t).wait_recv()
                    core_copy(last_slot, t).start()

        @pl.when((g == 0) & (seq == 0))
        def _():
            filter_copy().start()

        for side in range(2):
            for hop in hops:
                t = g - hop

                @pl.when((t >= 0) & (t < CHUNKS))
                def _(side=side, hop=hop, t=t):
                    if side == 1:
                        for slot in slots_at(hop):
                            core_copy(slot, t).wait_recv()
                    if side == 0 and hop == 0:
                        own_copy(t).wait()
                        acc[t] = product(side, hop, t)
                    else:
                        acc[t] += product(side, hop, t)

        @pl.when(g == full)
        def _():
            fwd_copy.wait()
            inv_copy.wait()
            lag_copy.wait()

            @pl.when(seq == 1)
            def _():
                filter_copy().wait_recv()

            spec[0] = nt_dot(fwd[...], lags[0])

            @pl.when(seq == 1)
            def _():
                sign = 1.0 - 2.0 * (
                    lax.broadcasted_iota(jnp.int32, (2 * rows, width), 0) % 2
                ).astype(F32)
                spec[1] = nt_dot(fwd[...], lags[1]) + sign * spec[0]

        done = g - far

        @pl.when(done >= 0)
        def _():
            for stream in range(3):
                cols = slice(stream * width, (stream + 1) * width)
                proj[stream, pl.ds(pl.multiple_of(done * size + HALO, HALO), size), :] = (
                    acc[done, :, cols].astype(BF16).astype(F32)
                )

            @pl.when((seq == 0) & (done == CHUNKS - 1))
            def _():
                halo_copy().start()

            @pl.when((seq == 0) | (done > 0))
            def _():
                gate(done)

            @pl.when(seq == 0)
            def _():
                gated_copy(done).start()

        return carry

    lax.fori_loop(0, CHUNKS + far, step, 0)

    @pl.when(seq == 1)
    def _():
        halo_copy().wait_recv()
        gate(0)

    first = lax.broadcasted_iota(jnp.int32, (rows, width), 0) == 0

    def term(lag, source):
        signal = jnp.dot(fwd[...], source[...], preferred_element_type=F32)
        return times(
            spec[lag, :rows], spec[lag, rows:], signal[:rows], signal[rows:], first
        )

    total[0], total[1] = term(0, gated)

    @pl.when(seq == 1)
    def _():
        for t in range(CHUNKS):
            gated_copy(t).wait_recv()
        real_part, imag_part = term(1, gated_in)
        total[0] += real_part
        total[1] += imag_part

    scale = jnp.where(first, 0.5, 1.0) / rows
    spectrum = jnp.concatenate(
        [(total[0] * scale).astype(BF16), (total[1] * scale).astype(BF16)], axis=0
    )
    conv = jnp.dot(inv[...], spectrum, preferred_element_type=F32)
    for t in range(CHUNKS):
        here = slice(t * size, (t + 1) * size)
        out[here, :] = (
            short(0, t) * (conv[here] + gain[...] * gated[here, :].astype(F32))
        ).astype(BF16)

    def finish(t, carry):
        for hop in range(1, far):
            for d in range(2):
                ring_copy(d, hop, t).wait_send()
        for d in range(2):

            @pl.when(t % 2 == d)
            def _(d=d):
                ring_copy(d, far, t).wait_send()

        for slot in range(last_slot + 1):
            core_copy(slot, t).wait_send()

        @pl.when(seq == 0)
        def _():
            gated_copy(t).wait_send()

        return carry

    lax.fori_loop(0, CHUNKS, finish, 0)

    @pl.when(seq == 0)
    def _():
        halo_copy().wait_send()
        filter_copy().wait_send()


def fused(chips, activations, in_weight, short_taps, long_filter, skip_gain):
    rows, depth = activations.shape
    width = in_weight.shape[1]
    forward, inverse = half_tables(rows)
    size = rows // CHUNKS
    here = pl.BlockSpec(memory_space=pltpu.VMEM)
    there = pl.BlockSpec(memory_space=pl.ANY)
    dma = pltpu.SemaphoreType.DMA
    return pl.pallas_call(
        functools.partial(fused_kernel, chips),
        out_shape=jax.ShapeDtypeStruct((rows, width), BF16),
        in_specs=[there, there, here, there, here, there, there],
        out_specs=here,
        scratch_shapes=[
            pltpu.VMEM((2, chips, CHUNKS, size, depth), BF16),
            pltpu.VMEM((2, chips, 3, width, depth), BF16),
            pltpu.VMEM((CHUNKS, size, 3 * width), F32),
            pltpu.VMEM((3, rows + HALO, width), F32),
            pltpu.VMEM((rows, width), BF16),
            pltpu.VMEM((rows, width), BF16),
            pltpu.VMEM((2, width, rows), BF16),
            pltpu.VMEM((2 * rows, rows), BF16),
            pltpu.VMEM((rows, 2 * rows), BF16),
            pltpu.VMEM((2, 2 * rows, width), F32),
            pltpu.VMEM((2, rows, width), F32),
            dma((chips, CHUNKS)),
            dma((chips, CHUNKS)),
            dma((chips, CHUNKS)),
            dma((chips, CHUNKS)),
            dma((CHUNKS,)),
            dma((2, chips)),
            dma((3,)),
            dma((CHUNKS + 2,)),
            dma((CHUNKS + 2,)),
        ],
        compiler_params=pltpu.CompilerParams(
            collective_id=0, has_side_effects=True, vmem_limit_bytes=48 * 1024 * 1024
        ),
        cost_estimate=pl.CostEstimate(
            flops=2 * rows * chips * 2 * depth * 3 * width,
            bytes_accessed=in_weight.size * 2,
            transcendentals=0,
        ),
    )(
        activations, in_weight, short_taps, long_filter, skip_gain[None, :],
        jnp.asarray(forward), jnp.asarray(inverse),
    )


def general(activations, in_weight, short_taps, long_filter, skip_gain):
    rows = activations.shape[0]
    channels = in_weight.shape[1]
    proj = jnp.einsum(
        "tk,sck->tsc",
        lax.all_gather(activations, "chan", axis=1, tiled=True),
        in_weight,
        preferred_element_type=F32,
    ).astype(BF16)
    earlier = from_behind(proj[rows - 2 :], "seq", 1)
    padded = jnp.concatenate([earlier, proj], axis=0).astype(F32)
    feat = (
        short_taps[:, 0, :] * padded[2:]
        + short_taps[:, 1, :] * padded[1:-1]
        + short_taps[:, 2, :] * padded[:-2]
    )
    gated = (feat[:, 1, :] * feat[:, 2, :]).astype(BF16)
    forward, inverse = (jnp.asarray(table) for table in half_tables(rows))
    seq_count = lax.axis_size("seq")
    all_lags = lax.all_gather(long_filter, "seq", axis=1, tiled=True)
    lag_blocks = all_lags.reshape(channels, seq_count, rows)
    spec = jnp.einsum("ft,cmt->mfc", forward, lag_blocks, preferred_element_type=F32)
    sign = (1.0 - 2.0 * (jnp.arange(2 * rows) % 2)).astype(F32)[:, None]
    spec = spec.at[1:].add(sign * spec[:-1])
    first = jnp.arange(rows)[:, None] == 0
    total = (jnp.zeros((rows, channels), F32), jnp.zeros((rows, channels), F32))
    moving = gated
    for section in range(seq_count):
        if section > 0:
            moving = from_behind(moving, "seq", 1)
        signal = jnp.dot(forward, moving, preferred_element_type=F32)
        part = times(
            spec[section, :rows], spec[section, rows:], signal[:rows], signal[rows:], first
        )
        total = (total[0] + part[0], total[1] + part[1])
    scale = jnp.where(first, 0.5, 1.0) / rows
    spectrum = jnp.concatenate([total[0] * scale, total[1] * scale], axis=0).astype(BF16)
    conv = jnp.dot(inverse, spectrum, preferred_element_type=F32)
    return (feat[:, 0, :] * (conv + skip_gain * gated.astype(F32))).astype(BF16)


def solution(mesh):
    in_specs = (
        P("seq", "chan"),
        P(None, "chan", None),
        P(None, None, "chan"),
        P("chan", "seq"),
        P("chan"),
    )
    out_specs = P("seq", "chan")
    chan = mesh.shape["chan"]
    if mesh.shape["seq"] == 2 and chan == 16:
        on_device = functools.partial(fused, chan // 2)
    else:
        on_device = general
    return jax.shard_map(
        on_device, mesh=mesh, in_specs=in_specs, out_specs=out_specs, check_vma=False
    )
```

```python
import functools
import math

import jax
import jax.numpy as jnp
import ml_dtypes
import numpy as np
from jax import lax
from jax.experimental import pallas as pl
from jax.experimental.pallas import tpu as pltpu
from jax.sharding import PartitionSpec as P

MESH = pl.DeviceIdType.MESH
F32 = jnp.float32
BF16 = jnp.bfloat16
CHUNKS = 4
HALO = 8


def from_behind(block, axis, distance):
    devices = range(lax.axis_size(axis))
    route = [(i - distance, i) for i in devices if i - distance in devices]
    return lax.ppermute(block, axis, route)


def half_tables(length):
    double = 2 * length
    index = np.arange(length, dtype=np.int64)
    phase = ((index[:, None] * index[None, :]) % double).astype(np.float32) * np.float32(
        2.0 * math.pi / double
    )
    cosine = np.cos(phase)
    sine = -np.sin(phase)
    sine[0] = 1.0 - 2.0 * (index % 2)
    forward = np.concatenate([cosine, sine], axis=0).astype(ml_dtypes.bfloat16)
    inverse = np.concatenate([cosine, sine.T], axis=1).astype(ml_dtypes.bfloat16)
    return forward, inverse


def times(fil_real, fil_imag, sig_real, sig_imag, first):
    cross = jnp.where(first, 0.0, fil_imag)
    real_part = fil_real * sig_real - cross * sig_imag
    imag_part = jnp.where(first, fil_imag, fil_real) * sig_imag + cross * sig_real
    return real_part, imag_part


def nt_dot(a, b):
    return lax.dot_general(a, b, (((1,), (1,)), ((), ())), preferred_element_type=F32)


def fused_kernel(
    chips, act, weight, taps_in, filt, gain_in, fwd_in, inv_in, out,
    blocks, wv, acc, proj, gated, gated_in, lags, fwd, inv, taps, gain, spec, total,
    ring_send, ring_recv, core_send, core_recv, own_sem, weight_sem, load_sem,
    seq_send, seq_recv,
):
    rows, depth = act.shape
    width = taps_in.shape[-1]
    size = rows // CHUNKS
    far = chips // 2
    full = far - 1
    last_slot = 2 * full + 1

    seq = lax.axis_index("seq")
    chan = lax.axis_index("chan")
    chip, core = chan // 2, chan % 2

    def chip_at(place):
        place = lax.rem(place + 2 * chips, chips)
        return jnp.where(place < far, 2 * place, 2 * (chips - 1 - place) + 1)

    place = jnp.where(chip % 2 == 0, chip // 2, chips - 1 - chip // 2)
    ahead = (chip_at(place + 1) * 2 + core, chip_at(place - 1) * 2 + core)
    sibling = chip * 2 + 1 - core

    def slot_of(d, hop):
        if hop == 0:
            return 0
        return last_slot if hop == far else 1 + d * full + hop - 1

    def slots_at(hop):
        return [slot_of(0, hop)] if hop in (0, far) else [slot_of(0, hop), slot_of(1, hop)]

    def chunk(t):
        return pl.ds(pl.multiple_of(t * size, size), size)

    def ring_copy(d, hop, t):
        src = act.at[chunk(t)] if hop == 1 else blocks.at[0, slot_of(d, hop - 1), t]
        slot = slot_of(d, hop)
        return pltpu.make_async_remote_copy(
            src_ref=src, dst_ref=blocks.at[0, slot, t],
            send_sem=ring_send.at[slot, t], recv_sem=ring_recv.at[slot, t],
            device_id=(seq, ahead[d]), device_id_type=MESH,
        )

    def core_copy(slot, t):
        src = act.at[chunk(t)] if slot == 0 else blocks.at[0, slot, t]
        return pltpu.make_async_remote_copy(
            src_ref=src, dst_ref=blocks.at[1, slot, t],
            send_sem=core_send.at[slot, t], recv_sem=core_recv.at[slot, t],
            device_id=(seq, sibling), device_id_type=MESH,
        )

    def seq_copy(src, dst, n):
        return pltpu.make_async_remote_copy(
            src_ref=src, dst_ref=dst, send_sem=seq_send.at[n], recv_sem=seq_recv.at[n],
            device_id=(1 - seq, chan), device_id_type=MESH,
        )

    def gated_copy(t):
        return seq_copy(gated.at[chunk(t)], gated_in.at[chunk(t)], t)

    def halo_copy():
        return seq_copy(proj.at[:, pl.ds(rows, HALO)], proj.at[:, pl.ds(0, HALO)], CHUNKS)

    def filter_copy():
        return seq_copy(filt, lags.at[0], CHUNKS + 1)

    def own_copy(t):
        return pltpu.make_async_copy(act.at[chunk(t)], blocks.at[0, 0, t], own_sem.at[t])

    def weight_copy(side, slot):
        if slot == 0:
            origin = chip
        elif slot == last_slot:
            origin = chip_at(place + far)
        elif slot <= full:
            origin = chip_at(place - slot)
        else:
            origin = chip_at(place + slot - full)
        block = origin * 2 + (core if side == 0 else 1 - core)
        cols = pl.ds(pl.multiple_of(block * depth, depth), depth)
        return pltpu.make_async_copy(
            weight.at[:, :, cols], wv.at[side, slot], weight_sem.at[side, slot]
        )

    fwd_copy = pltpu.make_async_copy(fwd_in, fwd, load_sem.at[0])
    inv_copy = pltpu.make_async_copy(inv_in, inv, load_sem.at[1])
    lag_copy = pltpu.make_async_copy(filt, lags.at[seq], load_sem.at[2])
    taps_copy = pltpu.make_async_copy(taps_in, taps, load_sem.at[3])
    gain_copy = pltpu.make_async_copy(gain_in, gain, load_sem.at[4])

    for t in range(CHUNKS):
        own_copy(t).start()
    for slot in range(last_slot + 1):
        for side in range(2):
            weight_copy(side, slot).start()
    lag_copy.start()
    fwd_copy.start()
    inv_copy.start()
    taps_copy.start()
    gain_copy.start()

    barrier = pltpu.get_barrier_semaphore()
    for target in ((seq, ahead[0]), (seq, ahead[1]), (seq, sibling), (1 - seq, chan)):
        pl.semaphore_signal(barrier, inc=1, device_id=target, device_id_type=MESH)
    pl.semaphore_wait(barrier, 4)

    @pl.when(seq == 0)
    def _():
        proj[:, pl.ds(0, HALO), :] = jnp.zeros((3, HALO, width), F32)

    def short(stream, t):
        window = proj[stream, pl.ds(pl.multiple_of(t * size, size), size + HALO), :]
        return (
            taps[stream, 0, :][None] * window[HALO:]
            + taps[stream, 1, :][None] * window[HALO - 1 : HALO - 1 + size]
            + taps[stream, 2, :][None] * window[HALO - 2 : HALO - 2 + size]
        )

    def gate(t):
        gated[chunk(t), :] = (short(1, t) * short(2, t)).astype(BF16)

    def product(hop, t):
        parts = [(side, slot) for side in range(2) for slot in slots_at(hop)]

        @pl.when(t == 1)
        def _():
            for side, slot in parts:
                weight_copy(side, slot).wait()

        x = jnp.concatenate(
            [
                blocks[side, slot, pl.ds(t - 1, 2)].reshape(2 * size, depth)
                for side, slot in parts
            ],
            axis=1,
        )
        w = jnp.concatenate(
            [wv[side, slot].reshape(3 * width, depth) for side, slot in parts], axis=1
        )
        return nt_dot(x, w)

    hops = list(range(far, -1, -1))

    def step(g, carry):
        for hop in hops:
            t = g - hop

            @pl.when((t >= 0) & (t < CHUNKS))
            def _(hop=hop, t=t):
                if hop == 0:
                    for d in range(2):
                        ring_copy(d, 1, t).start()
                    core_copy(0, t).start()
                elif hop < far:
                    for d in range(2):
                        ring_copy(d, hop, t).wait_recv()
                        if hop < full:
                            ring_copy(d, hop + 1, t).start()
                        else:

                            @pl.when(t % 2 == d)
                            def _(d=d):
                                ring_copy(d, far, t).start()

                        core_copy(slot_of(d, hop), t).start()
                else:
                    ring_copy(0, far, t).wait_recv()
                    core_copy(last_slot, t).start()

        @pl.when((g == 0) & (seq == 0))
        def _():
            filter_copy().start()

        for hop in hops:
            t = g - 1 - hop

            @pl.when((t >= 0) & (t < CHUNKS) & (t % 2 == 1))
            def _(hop=hop, t=t):
                for slot in slots_at(hop):
                    core_copy(slot, t - 1).wait_recv()
                    core_copy(slot, t).wait_recv()
                if hop == 0:
                    own_copy(t - 1).wait()
                    own_copy(t).wait()
                    acc[t // 2] = product(hop, t)
                else:
                    acc[t // 2] += product(hop, t)

        @pl.when(g == full)
        def _():
            fwd_copy.wait()
            inv_copy.wait()
            lag_copy.wait()
            taps_copy.wait()
            gain_copy.wait()

            @pl.when(seq == 1)
            def _():
                filter_copy().wait_recv()

            spec[0] = nt_dot(fwd[...], lags[0])

            @pl.when(seq == 1)
            def _():
                sign = 1.0 - 2.0 * (
                    lax.broadcasted_iota(jnp.int32, (2 * rows, width), 0) % 2
                ).astype(F32)
                spec[1] = nt_dot(fwd[...], lags[1]) + sign * spec[0]

        done = g - 1 - far

        @pl.when((done >= 0) & (done % 2 == 1))
        def _():
            for stream in range(3):
                cols = slice(stream * width, (stream + 1) * width)
                start = pl.multiple_of((done - 1) * size + HALO, HALO)
                proj[stream, pl.ds(start, 2 * size), :] = (
                    acc[done // 2, :, cols].astype(BF16).astype(F32)
                )

            @pl.when((seq == 0) & (done == CHUNKS - 1))
            def _():
                halo_copy().start()

            for t in (done - 1, done):

                @pl.when((seq == 0) | (t > 0))
                def _(t=t):
                    gate(t)

                @pl.when(seq == 0)
                def _(t=t):
                    gated_copy(t).start()

        return carry

    lax.fori_loop(0, CHUNKS + far + 1, step, 0)

    @pl.when(seq == 1)
    def _():
        halo_copy().wait_recv()
        gate(0)

    first = lax.broadcasted_iota(jnp.int32, (rows, width), 0) == 0

    def term(lag, source):
        signal = jnp.dot(fwd[...], source[...], preferred_element_type=F32)
        return times(
            spec[lag, :rows], spec[lag, rows:], signal[:rows], signal[rows:], first
        )

    total[0], total[1] = term(0, gated)

    @pl.when(seq == 1)
    def _():
        for t in range(CHUNKS):
            gated_copy(t).wait_recv()
        real_part, imag_part = term(1, gated_in)
        total[0] += real_part
        total[1] += imag_part

    scale = jnp.where(first, 0.5, 1.0) / rows
    spectrum = jnp.concatenate(
        [(total[0] * scale).astype(BF16), (total[1] * scale).astype(BF16)], axis=0
    )
    conv = jnp.dot(inv[...], spectrum, preferred_element_type=F32)
    for t in range(CHUNKS):
        here = slice(t * size, (t + 1) * size)
        out[here, :] = (
            short(0, t) * (conv[here] + gain[...] * gated[here, :].astype(F32))
        ).astype(BF16)

    def finish(t, carry):
        for hop in range(1, far):
            for d in range(2):
                ring_copy(d, hop, t).wait_send()
        for d in range(2):

            @pl.when(t % 2 == d)
            def _(d=d):
                ring_copy(d, far, t).wait_send()

        for slot in range(last_slot + 1):
            core_copy(slot, t).wait_send()

        @pl.when(seq == 0)
        def _():
            gated_copy(t).wait_send()

        return carry

    lax.fori_loop(0, CHUNKS, finish, 0)

    @pl.when(seq == 0)
    def _():
        halo_copy().wait_send()
        filter_copy().wait_send()


def fused(chips, activations, in_weight, short_taps, long_filter, skip_gain):
    rows, depth = activations.shape
    width = in_weight.shape[1]
    forward, inverse = half_tables(rows)
    size = rows // CHUNKS
    here = pl.BlockSpec(memory_space=pltpu.VMEM)
    there = pl.BlockSpec(memory_space=pltpu.HBM)
    dma = pltpu.SemaphoreType.DMA
    return pl.pallas_call(
        functools.partial(fused_kernel, chips),
        out_shape=jax.ShapeDtypeStruct((rows, width), BF16),
        in_specs=[there] * 7,
        out_specs=here,
        scratch_shapes=[
            pltpu.VMEM((2, chips, CHUNKS, size, depth), BF16),
            pltpu.VMEM((2, chips, 3, width, depth), BF16),
            pltpu.VMEM((CHUNKS // 2, 2 * size, 3 * width), F32),
            pltpu.VMEM((3, rows + HALO, width), F32),
            pltpu.VMEM((rows, width), BF16),
            pltpu.VMEM((rows, width), BF16),
            pltpu.VMEM((2, width, rows), BF16),
            pltpu.VMEM((2 * rows, rows), BF16),
            pltpu.VMEM((rows, 2 * rows), BF16),
            pltpu.VMEM((3, 3, width), F32),
            pltpu.VMEM((1, width), F32),
            pltpu.VMEM((2, 2 * rows, width), F32),
            pltpu.VMEM((2, rows, width), F32),
            dma((chips, CHUNKS)),
            dma((chips, CHUNKS)),
            dma((chips, CHUNKS)),
            dma((chips, CHUNKS)),
            dma((CHUNKS,)),
            dma((2, chips)),
            dma((5,)),
            dma((CHUNKS + 2,)),
            dma((CHUNKS + 2,)),
        ],
        compiler_params=pltpu.CompilerParams(
            collective_id=0, has_side_effects=True, vmem_limit_bytes=63 * 1024 * 1024
        ),
        cost_estimate=pl.CostEstimate(
            flops=2 * rows * chips * 2 * depth * 3 * width,
            bytes_accessed=in_weight.size * 2,
            transcendentals=0,
        ),
    )(
        activations, in_weight, short_taps, long_filter, skip_gain[None, :],
        jnp.asarray(forward), jnp.asarray(inverse),
    )


def general(activations, in_weight, short_taps, long_filter, skip_gain):
    rows = activations.shape[0]
    channels = in_weight.shape[1]
    proj = jnp.einsum(
        "tk,sck->tsc",
        lax.all_gather(activations, "chan", axis=1, tiled=True),
        in_weight,
        preferred_element_type=F32,
    ).astype(BF16)
    earlier = from_behind(proj[rows - 2 :], "seq", 1)
    padded = jnp.concatenate([earlier, proj], axis=0).astype(F32)
    feat = (
        short_taps[:, 0, :] * padded[2:]
        + short_taps[:, 1, :] * padded[1:-1]
        + short_taps[:, 2, :] * padded[:-2]
    )
    gated = (feat[:, 1, :] * feat[:, 2, :]).astype(BF16)
    forward, inverse = (jnp.asarray(table) for table in half_tables(rows))
    seq_count = lax.axis_size("seq")
    all_lags = lax.all_gather(long_filter, "seq", axis=1, tiled=True)
    lag_blocks = all_lags.reshape(channels, seq_count, rows)
    spec = jnp.einsum("ft,cmt->mfc", forward, lag_blocks, preferred_element_type=F32)
    sign = (1.0 - 2.0 * (jnp.arange(2 * rows) % 2)).astype(F32)[:, None]
    spec = spec.at[1:].add(sign * spec[:-1])
    first = jnp.arange(rows)[:, None] == 0
    total = (jnp.zeros((rows, channels), F32), jnp.zeros((rows, channels), F32))
    moving = gated
    for section in range(seq_count):
        if section > 0:
            moving = from_behind(moving, "seq", 1)
        signal = jnp.dot(forward, moving, preferred_element_type=F32)
        part = times(
            spec[section, :rows], spec[section, rows:], signal[:rows], signal[rows:], first
        )
        total = (total[0] + part[0], total[1] + part[1])
    scale = jnp.where(first, 0.5, 1.0) / rows
    spectrum = jnp.concatenate([total[0] * scale, total[1] * scale], axis=0).astype(BF16)
    conv = jnp.dot(inverse, spectrum, preferred_element_type=F32)
    return (feat[:, 0, :] * (conv + skip_gain * gated.astype(F32))).astype(BF16)


def solution(mesh):
    in_specs = (
        P("seq", "chan"),
        P(None, "chan", None),
        P(None, None, "chan"),
        P("chan", "seq"),
        P("chan"),
    )
    out_specs = P("seq", "chan")
    chan = mesh.shape["chan"]
    if mesh.shape["seq"] == 2 and chan == 16:
        on_device = functools.partial(fused, chan // 2)
    else:
        on_device = general
    return jax.shard_map(
        on_device, mesh=mesh, in_specs=in_specs, out_specs=out_specs, check_vma=False
    )
```

```python
import functools
import math

import jax
import jax.numpy as jnp
import ml_dtypes
import numpy as np
from jax import lax
from jax.experimental import pallas as pl
from jax.experimental.pallas import tpu as pltpu
from jax.sharding import PartitionSpec as P

MESH = pl.DeviceIdType.MESH
F32 = jnp.float32
BF16 = jnp.bfloat16
CHUNKS = 4
HALO = 8


def from_behind(block, axis, distance):
    devices = range(lax.axis_size(axis))
    route = [(i - distance, i) for i in devices if i - distance in devices]
    return lax.ppermute(block, axis, route)


def half_tables(length):
    double = 2 * length
    index = np.arange(length, dtype=np.int64)
    phase = ((index[:, None] * index[None, :]) % double).astype(np.float32) * np.float32(
        2.0 * math.pi / double
    )
    cosine = np.cos(phase)
    sine = -np.sin(phase)
    sine[0] = 1.0 - 2.0 * (index % 2)
    forward = np.concatenate([cosine, sine], axis=0).astype(ml_dtypes.bfloat16)
    inverse = np.concatenate([cosine, sine.T], axis=1).astype(ml_dtypes.bfloat16)
    return forward, inverse


def times(fil_real, fil_imag, sig_real, sig_imag, first):
    cross = jnp.where(first, 0.0, fil_imag)
    real_part = fil_real * sig_real - cross * sig_imag
    imag_part = jnp.where(first, fil_imag, fil_real) * sig_imag + cross * sig_real
    return real_part, imag_part


def nt_dot(a, b):
    return lax.dot_general(a, b, (((1,), (1,)), ((), ())), preferred_element_type=F32)


def fused_kernel(
    chips, act, weight, taps_in, filt, gain_in, fwd_in, inv_in, out,
    blocks, wv, acc, proj, gated, gated_in, lags, fwd, inv, taps, gain, spec, total,
    ring_send, ring_recv, core_send, core_recv, own_sem, weight_sem, load_sem,
    seq_send, seq_recv,
):
    rows, depth = act.shape
    width = taps_in.shape[-1]
    size = rows // CHUNKS
    far = chips // 2
    full = far - 1
    last_slot = 2 * full + 1

    seq = lax.axis_index("seq")
    chan = lax.axis_index("chan")
    chip, core = chan // 2, chan % 2

    def chip_at(place):
        place = lax.rem(place + 2 * chips, chips)
        return jnp.where(place < far, 2 * place, 2 * (chips - 1 - place) + 1)

    place = jnp.where(chip % 2 == 0, chip // 2, chips - 1 - chip // 2)
    ahead = (chip_at(place + 1) * 2 + core, chip_at(place - 1) * 2 + core)
    sibling = chip * 2 + 1 - core

    def slot_of(d, hop):
        if hop == 0:
            return 0
        return last_slot if hop == far else 1 + d * full + hop - 1

    def slots_at(hop):
        return [slot_of(0, hop)] if hop in (0, far) else [slot_of(0, hop), slot_of(1, hop)]

    def chunk(t):
        return pl.ds(pl.multiple_of(t * size, size), size)

    def ring_copy(d, hop, t):
        src = act.at[chunk(t)] if hop == 1 else blocks.at[0, slot_of(d, hop - 1), t]
        slot = slot_of(d, hop)
        return pltpu.make_async_remote_copy(
            src_ref=src, dst_ref=blocks.at[0, slot, t],
            send_sem=ring_send.at[slot, t], recv_sem=ring_recv.at[slot, t],
            device_id=(seq, ahead[d]), device_id_type=MESH,
        )

    def core_copy(slot, t):
        src = act.at[chunk(t)] if slot == 0 else blocks.at[0, slot, t]
        return pltpu.make_async_remote_copy(
            src_ref=src, dst_ref=blocks.at[1, slot, t],
            send_sem=core_send.at[slot, t], recv_sem=core_recv.at[slot, t],
            device_id=(seq, sibling), device_id_type=MESH,
        )

    def seq_copy(src, dst, n):
        return pltpu.make_async_remote_copy(
            src_ref=src, dst_ref=dst, send_sem=seq_send.at[n], recv_sem=seq_recv.at[n],
            device_id=(1 - seq, chan), device_id_type=MESH,
        )

    def gated_copy(t):
        return seq_copy(gated.at[chunk(t)], gated_in.at[chunk(t)], t)

    def halo_copy():
        return seq_copy(proj.at[:, pl.ds(rows, HALO)], proj.at[:, pl.ds(0, HALO)], CHUNKS)

    def filter_copy():
        return seq_copy(filt, lags.at[0], CHUNKS + 1)

    def own_copy(t):
        return pltpu.make_async_copy(act.at[chunk(t)], blocks.at[0, 0, t], own_sem.at[t])

    def weight_copy(side, slot):
        if slot == 0:
            origin = chip
        elif slot == last_slot:
            origin = chip_at(place + far)
        elif slot <= full:
            origin = chip_at(place - slot)
        else:
            origin = chip_at(place + slot - full)
        block = origin * 2 + (core if side == 0 else 1 - core)
        cols = pl.ds(pl.multiple_of(block * depth, depth), depth)
        return pltpu.make_async_copy(
            weight.at[:, :, cols], wv.at[side, slot], weight_sem.at[side, slot]
        )

    fwd_copy = pltpu.make_async_copy(fwd_in, fwd, load_sem.at[0])
    inv_copy = pltpu.make_async_copy(inv_in, inv, load_sem.at[1])
    lag_copy = pltpu.make_async_copy(filt, lags.at[seq], load_sem.at[2])
    taps_copy = pltpu.make_async_copy(taps_in, taps, load_sem.at[3])
    gain_copy = pltpu.make_async_copy(gain_in, gain, load_sem.at[4])

    for t in range(CHUNKS):
        own_copy(t).start()
    for slot in range(last_slot + 1):
        for side in range(2):
            weight_copy(side, slot).start()
    lag_copy.start()
    fwd_copy.start()
    inv_copy.start()
    taps_copy.start()
    gain_copy.start()

    barrier = pltpu.get_barrier_semaphore()
    for target in ((seq, ahead[0]), (seq, ahead[1]), (seq, sibling), (1 - seq, chan)):
        pl.semaphore_signal(barrier, inc=1, device_id=target, device_id_type=MESH)
    pl.semaphore_wait(barrier, 4)

    @pl.when(seq == 0)
    def _():
        proj[:, pl.ds(0, HALO), :] = jnp.zeros((3, HALO, width), F32)

    def short(stream, t):
        window = proj[stream, pl.ds(pl.multiple_of(t * size, size), size + HALO), :]
        return (
            taps[stream, 0, :][None] * window[HALO:]
            + taps[stream, 1, :][None] * window[HALO - 1 : HALO - 1 + size]
            + taps[stream, 2, :][None] * window[HALO - 2 : HALO - 2 + size]
        )

    def gate(t):
        gated[chunk(t), :] = (short(1, t) * short(2, t)).astype(BF16)

    def product(hop, t):
        parts = [(side, slot) for side in range(2) for slot in slots_at(hop)]

        @pl.when(t == 1)
        def _():
            for side, slot in parts:
                weight_copy(side, slot).wait()

        x = jnp.concatenate(
            [
                blocks[side, slot, pl.ds(t - 1, 2)].reshape(2 * size, depth)
                for side, slot in parts
            ],
            axis=1,
        )
        w = jnp.concatenate(
            [wv[side, slot].reshape(3 * width, depth) for side, slot in parts], axis=1
        )
        return nt_dot(w, x)

    hops = list(range(far, -1, -1))

    def step(g, carry):
        for hop in hops:
            t = g - hop

            @pl.when((t >= 0) & (t < CHUNKS))
            def _(hop=hop, t=t):
                if hop == 0:
                    for d in range(2):
                        ring_copy(d, 1, t).start()
                    core_copy(0, t).start()
                elif hop < far:
                    for d in range(2):
                        ring_copy(d, hop, t).wait_recv()
                        if hop < full:
                            ring_copy(d, hop + 1, t).start()
                        else:

                            @pl.when(t % 2 == d)
                            def _(d=d):
                                ring_copy(d, far, t).start()

                        core_copy(slot_of(d, hop), t).start()
                else:
                    ring_copy(0, far, t).wait_recv()
                    core_copy(last_slot, t).start()

        @pl.when((g == 0) & (seq == 0))
        def _():
            filter_copy().start()

        for hop in hops:
            t = g - 1 - hop

            @pl.when((t >= 0) & (t < CHUNKS) & (t % 2 == 1))
            def _(hop=hop, t=t):
                for slot in slots_at(hop):
                    core_copy(slot, t - 1).wait_recv()
                    core_copy(slot, t).wait_recv()
                if hop == 0:
                    own_copy(t - 1).wait()
                    own_copy(t).wait()
                    acc[t // 2] = product(hop, t)
                else:
                    acc[t // 2] += product(hop, t)

        @pl.when(g == full)
        def _():
            fwd_copy.wait()
            inv_copy.wait()
            lag_copy.wait()
            taps_copy.wait()
            gain_copy.wait()

            @pl.when(seq == 1)
            def _():
                filter_copy().wait_recv()

            spec[0] = nt_dot(fwd[...], lags[0])

            @pl.when(seq == 1)
            def _():
                sign = 1.0 - 2.0 * (
                    lax.broadcasted_iota(jnp.int32, (2 * rows, width), 0) % 2
                ).astype(F32)
                spec[1] = nt_dot(fwd[...], lags[1]) + sign * spec[0]

        done = g - 1 - far

        @pl.when((done >= 0) & (done % 2 == 1))
        def _():
            for stream in range(3):
                cols = slice(stream * width, (stream + 1) * width)
                start = pl.multiple_of((done - 1) * size + HALO, HALO)
                proj[stream, pl.ds(start, 2 * size), :] = (
                    acc[done // 2, cols, :].astype(BF16).T.astype(F32)
                )

            @pl.when((seq == 0) & (done == CHUNKS - 1))
            def _():
                halo_copy().start()

            for t in (done - 1, done):

                @pl.when((seq == 0) | (t > 0))
                def _(t=t):
                    gate(t)

                @pl.when(seq == 0)
                def _(t=t):
                    gated_copy(t).start()

        return carry

    lax.fori_loop(0, CHUNKS + far + 1, step, 0)

    @pl.when(seq == 1)
    def _():
        halo_copy().wait_recv()
        gate(0)

    first = lax.broadcasted_iota(jnp.int32, (rows, width), 0) == 0

    def term(lag, source):
        signal = jnp.dot(fwd[...], source[...], preferred_element_type=F32)
        return times(
            spec[lag, :rows], spec[lag, rows:], signal[:rows], signal[rows:], first
        )

    total[0], total[1] = term(0, gated)

    @pl.when(seq == 1)
    def _():
        for t in range(CHUNKS):
            gated_copy(t).wait_recv()
        real_part, imag_part = term(1, gated_in)
        total[0] += real_part
        total[1] += imag_part

    scale = jnp.where(first, 0.5, 1.0) / rows
    spectrum = jnp.concatenate(
        [(total[0] * scale).astype(BF16), (total[1] * scale).astype(BF16)], axis=0
    )
    conv = jnp.dot(inv[...], spectrum, preferred_element_type=F32)
    for t in range(CHUNKS):
        here = slice(t * size, (t + 1) * size)
        out[here, :] = (
            short(0, t) * (conv[here] + gain[...] * gated[here, :].astype(F32))
        ).astype(BF16)

    def finish(t, carry):
        for hop in range(1, far):
            for d in range(2):
                ring_copy(d, hop, t).wait_send()
        for d in range(2):

            @pl.when(t % 2 == d)
            def _(d=d):
                ring_copy(d, far, t).wait_send()

        for slot in range(last_slot + 1):
            core_copy(slot, t).wait_send()

        @pl.when(seq == 0)
        def _():
            gated_copy(t).wait_send()

        return carry

    lax.fori_loop(0, CHUNKS, finish, 0)

    @pl.when(seq == 0)
    def _():
        halo_copy().wait_send()
        filter_copy().wait_send()


def fused(chips, activations, in_weight, short_taps, long_filter, skip_gain):
    rows, depth = activations.shape
    width = in_weight.shape[1]
    forward, inverse = half_tables(rows)
    size = rows // CHUNKS
    here = pl.BlockSpec(memory_space=pltpu.VMEM)
    there = pl.BlockSpec(memory_space=pltpu.HBM)
    dma = pltpu.SemaphoreType.DMA
    return pl.pallas_call(
        functools.partial(fused_kernel, chips),
        out_shape=jax.ShapeDtypeStruct((rows, width), BF16),
        in_specs=[there] * 7,
        out_specs=here,
        scratch_shapes=[
            pltpu.VMEM((2, chips, CHUNKS, size, depth), BF16),
            pltpu.VMEM((2, chips, 3, width, depth), BF16),
            pltpu.VMEM((CHUNKS // 2, 3 * width, 2 * size), F32),
            pltpu.VMEM((3, rows + HALO, width), F32),
            pltpu.VMEM((rows, width), BF16),
            pltpu.VMEM((rows, width), BF16),
            pltpu.VMEM((2, width, rows), BF16),
            pltpu.VMEM((2 * rows, rows), BF16),
            pltpu.VMEM((rows, 2 * rows), BF16),
            pltpu.VMEM((3, 3, width), F32),
            pltpu.VMEM((1, width), F32),
            pltpu.VMEM((2, 2 * rows, width), F32),
            pltpu.VMEM((2, rows, width), F32),
            dma((chips, CHUNKS)),
            dma((chips, CHUNKS)),
            dma((chips, CHUNKS)),
            dma((chips, CHUNKS)),
            dma((CHUNKS,)),
            dma((2, chips)),
            dma((5,)),
            dma((CHUNKS + 2,)),
            dma((CHUNKS + 2,)),
        ],
        compiler_params=pltpu.CompilerParams(
            collective_id=0, has_side_effects=True, vmem_limit_bytes=63 * 1024 * 1024
        ),
        cost_estimate=pl.CostEstimate(
            flops=2 * rows * chips * 2 * depth * 3 * width,
            bytes_accessed=in_weight.size * 2,
            transcendentals=0,
        ),
    )(
        activations, in_weight, short_taps, long_filter, skip_gain[None, :],
        jnp.asarray(forward), jnp.asarray(inverse),
    )


def general(activations, in_weight, short_taps, long_filter, skip_gain):
    rows = activations.shape[0]
    channels = in_weight.shape[1]
    proj = jnp.einsum(
        "tk,sck->tsc",
        lax.all_gather(activations, "chan", axis=1, tiled=True),
        in_weight,
        preferred_element_type=F32,
    ).astype(BF16)
    earlier = from_behind(proj[rows - 2 :], "seq", 1)
    padded = jnp.concatenate([earlier, proj], axis=0).astype(F32)
    feat = (
        short_taps[:, 0, :] * padded[2:]
        + short_taps[:, 1, :] * padded[1:-1]
        + short_taps[:, 2, :] * padded[:-2]
    )
    gated = (feat[:, 1, :] * feat[:, 2, :]).astype(BF16)
    forward, inverse = (jnp.asarray(table) for table in half_tables(rows))
    seq_count = lax.axis_size("seq")
    all_lags = lax.all_gather(long_filter, "seq", axis=1, tiled=True)
    lag_blocks = all_lags.reshape(channels, seq_count, rows)
    spec = jnp.einsum("ft,cmt->mfc", forward, lag_blocks, preferred_element_type=F32)
    sign = (1.0 - 2.0 * (jnp.arange(2 * rows) % 2)).astype(F32)[:, None]
    spec = spec.at[1:].add(sign * spec[:-1])
    first = jnp.arange(rows)[:, None] == 0
    total = (jnp.zeros((rows, channels), F32), jnp.zeros((rows, channels), F32))
    moving = gated
    for section in range(seq_count):
        if section > 0:
            moving = from_behind(moving, "seq", 1)
        signal = jnp.dot(forward, moving, preferred_element_type=F32)
        part = times(
            spec[section, :rows], spec[section, rows:], signal[:rows], signal[rows:], first
        )
        total = (total[0] + part[0], total[1] + part[1])
    scale = jnp.where(first, 0.5, 1.0) / rows
    spectrum = jnp.concatenate([total[0] * scale, total[1] * scale], axis=0).astype(BF16)
    conv = jnp.dot(inverse, spectrum, preferred_element_type=F32)
    return (feat[:, 0, :] * (conv + skip_gain * gated.astype(F32))).astype(BF16)


def solution(mesh):
    in_specs = (
        P("seq", "chan"),
        P(None, "chan", None),
        P(None, None, "chan"),
        P("chan", "seq"),
        P("chan"),
    )
    out_specs = P("seq", "chan")
    chan = mesh.shape["chan"]
    if mesh.shape["seq"] == 2 and chan == 16:
        on_device = functools.partial(fused, chan // 2)
    else:
        on_device = general
    return jax.shard_map(
        on_device, mesh=mesh, in_specs=in_specs, out_specs=out_specs, check_vma=False
    )
```

```python
import functools
import math

import jax
import jax.numpy as jnp
import ml_dtypes
import numpy as np
from jax import lax
from jax.experimental import pallas as pl
from jax.experimental.pallas import tpu as pltpu
from jax.sharding import PartitionSpec as P

MESH = pl.DeviceIdType.MESH
F32 = jnp.float32
BF16 = jnp.bfloat16
CHUNKS = 4
HALO = 8


def from_behind(block, axis, distance):
    devices = range(lax.axis_size(axis))
    route = [(i - distance, i) for i in devices if i - distance in devices]
    return lax.ppermute(block, axis, route)


def half_tables(length):
    double = 2 * length
    index = np.arange(length, dtype=np.int64)
    phase = ((index[:, None] * index[None, :]) % double).astype(np.float32) * np.float32(
        2.0 * math.pi / double
    )
    cosine = np.cos(phase)
    sine = -np.sin(phase)
    sine[0] = 1.0 - 2.0 * (index % 2)
    forward = np.concatenate([cosine, sine], axis=0).astype(ml_dtypes.bfloat16)
    inverse = np.concatenate([cosine, sine.T], axis=1).astype(ml_dtypes.bfloat16)
    return forward, inverse


def times(fil_real, fil_imag, sig_real, sig_imag, first):
    cross = jnp.where(first, 0.0, fil_imag)
    real_part = fil_real * sig_real - cross * sig_imag
    imag_part = jnp.where(first, fil_imag, fil_real) * sig_imag + cross * sig_real
    return real_part, imag_part


def nt_dot(a, b):
    return lax.dot_general(a, b, (((1,), (1,)), ((), ())), preferred_element_type=F32)


def fused_kernel(
    chips, act, weight, taps_in, filt, gain_in, fwd_in, inv_in, out,
    blocks, wv, acc, proj, gated, gated_in, lags, fwd, inv, taps, gain, spec, total,
    ring_send, ring_recv, core_send, core_recv, own_sem, weight_sem, load_sem,
    seq_send, seq_recv,
):
    rows, depth = act.shape
    width = taps_in.shape[-1]
    size = rows // CHUNKS
    far = chips // 2
    full = far - 1
    last_slot = 2 * full + 1

    seq = lax.axis_index("seq")
    chan = lax.axis_index("chan")
    chip, core = chan // 2, chan % 2

    def chip_at(place):
        place = lax.rem(place + 2 * chips, chips)
        return jnp.where(place < far, 2 * place, 2 * (chips - 1 - place) + 1)

    place = jnp.where(chip % 2 == 0, chip // 2, chips - 1 - chip // 2)
    ahead = (chip_at(place + 1) * 2 + core, chip_at(place - 1) * 2 + core)
    sibling = chip * 2 + 1 - core

    def slot_of(d, hop):
        if hop == 0:
            return 0
        return last_slot if hop == far else 1 + d * full + hop - 1

    def slots_at(hop):
        return [slot_of(0, hop)] if hop in (0, far) else [slot_of(0, hop), slot_of(1, hop)]

    def chunk(t):
        return pl.ds(pl.multiple_of(t * size, size), size)

    def ring_copy(d, hop, t):
        src = act.at[chunk(t)] if hop == 1 else blocks.at[0, slot_of(d, hop - 1), t]
        slot = slot_of(d, hop)
        return pltpu.make_async_remote_copy(
            src_ref=src, dst_ref=blocks.at[0, slot, t],
            send_sem=ring_send.at[slot, t], recv_sem=ring_recv.at[slot, t],
            device_id=(seq, ahead[d]), device_id_type=MESH,
        )

    def core_copy(slot, t):
        src = act.at[chunk(t)] if slot == 0 else blocks.at[0, slot, t]
        return pltpu.make_async_remote_copy(
            src_ref=src, dst_ref=blocks.at[1, slot, t],
            send_sem=core_send.at[slot, t], recv_sem=core_recv.at[slot, t],
            device_id=(seq, sibling), device_id_type=MESH,
        )

    def seq_copy(src, dst, n):
        return pltpu.make_async_remote_copy(
            src_ref=src, dst_ref=dst, send_sem=seq_send.at[n], recv_sem=seq_recv.at[n],
            device_id=(1 - seq, chan), device_id_type=MESH,
        )

    def gated_copy(t):
        return seq_copy(gated.at[chunk(t)], gated_in.at[chunk(t)], t)

    def halo_copy():
        return seq_copy(proj.at[:, pl.ds(rows, HALO)], proj.at[:, pl.ds(0, HALO)], CHUNKS)

    def filter_copy():
        return seq_copy(filt, lags.at[0], CHUNKS + 1)

    def own_copy(t):
        return pltpu.make_async_copy(act.at[chunk(t)], blocks.at[0, 0, t], own_sem.at[t])

    def weight_copy(side, slot):
        if slot == 0:
            origin = chip
        elif slot == last_slot:
            origin = chip_at(place + far)
        elif slot <= full:
            origin = chip_at(place - slot)
        else:
            origin = chip_at(place + slot - full)
        block = origin * 2 + (core if side == 0 else 1 - core)
        cols = pl.ds(pl.multiple_of(block * depth, depth), depth)
        return pltpu.make_async_copy(
            weight.at[:, :, cols], wv.at[side, slot], weight_sem.at[side, slot]
        )

    fwd_copy = pltpu.make_async_copy(fwd_in, fwd, load_sem.at[0])
    inv_copy = pltpu.make_async_copy(inv_in, inv, load_sem.at[1])
    lag_copy = pltpu.make_async_copy(filt, lags.at[seq], load_sem.at[2])
    taps_copy = pltpu.make_async_copy(taps_in, taps, load_sem.at[3])
    gain_copy = pltpu.make_async_copy(gain_in, gain, load_sem.at[4])

    for t in range(CHUNKS):
        own_copy(t).start()
    for slot in range(last_slot + 1):
        for side in range(2):
            weight_copy(side, slot).start()
    lag_copy.start()
    fwd_copy.start()
    inv_copy.start()
    taps_copy.start()
    gain_copy.start()

    barrier = pltpu.get_barrier_semaphore()
    for target in ((seq, ahead[0]), (seq, ahead[1]), (seq, sibling), (1 - seq, chan)):
        pl.semaphore_signal(barrier, inc=1, device_id=target, device_id_type=MESH)
    pl.semaphore_wait(barrier, 4)

    @pl.when(seq == 0)
    def _():
        proj[:, pl.ds(0, HALO), :] = jnp.zeros((3, HALO, width), F32)

    def short(stream, t):
        window = proj[stream, pl.ds(pl.multiple_of(t * size, size), size + HALO), :]
        return (
            taps[stream, 0, :][None] * window[HALO:]
            + taps[stream, 1, :][None] * window[HALO - 1 : HALO - 1 + size]
            + taps[stream, 2, :][None] * window[HALO - 2 : HALO - 2 + size]
        )

    def gate(t):
        gated[chunk(t), :] = (short(1, t) * short(2, t)).astype(BF16)

    def product(hop, t):
        parts = [(side, slot) for side in range(2) for slot in slots_at(hop)]

        @pl.when(t == 1)
        def _():
            for side, slot in parts:
                weight_copy(side, slot).wait()

        x = jnp.concatenate(
            [
                blocks[side, slot, pl.ds(t - 1, 2)].reshape(2 * size, depth)
                for side, slot in parts
            ],
            axis=1,
        )
        w = jnp.concatenate(
            [wv[side, slot].reshape(3 * width, depth) for side, slot in parts], axis=1
        )
        return nt_dot(w, x)

    def pass_on(hop, t):
        for d in range(2):
            if hop < far:
                ring_copy(d, hop, t).wait_recv()
                if hop < full:
                    ring_copy(d, hop + 1, t).start()
                else:

                    @pl.when(t % 2 == d)
                    def _(d=d):
                        ring_copy(d, far, t).start()

        if hop == far:
            ring_copy(0, far, t).wait_recv()
        for slot in slots_at(hop):
            core_copy(slot, t).start()

    def project(hop, t):
        for slot in slots_at(hop):
            core_copy(slot, t - 1).wait_recv()
            core_copy(slot, t).wait_recv()
        if hop == 0:
            own_copy(t - 1).wait()
            own_copy(t).wait()
            acc[t // 2] = product(hop, t)
        else:
            acc[t // 2] += product(hop, t)

    def finalize(done):
        for stream in range(3):
            cols = slice(stream * width, (stream + 1) * width)
            start = pl.multiple_of((done - 1) * size + HALO, HALO)
            proj[stream, pl.ds(start, 2 * size), :] = (
                acc[done // 2, cols, :].astype(BF16).T.astype(F32)
            )

        @pl.when((seq == 0) & (done == CHUNKS - 1))
        def _():
            halo_copy().start()

        for t in (done - 1, done):

            @pl.when((seq == 0) | (t > 0))
            def _(t=t):
                gate(t)

            @pl.when(seq == 0)
            def _(t=t):
                gated_copy(t).start()

    def filter_spectra():
        fwd_copy.wait()
        inv_copy.wait()
        lag_copy.wait()
        taps_copy.wait()
        gain_copy.wait()

        @pl.when(seq == 1)
        def _():
            filter_copy().wait_recv()

        spec[0] = nt_dot(fwd[...], lags[0])

        @pl.when(seq == 1)
        def _():
            sign = 1.0 - 2.0 * (
                lax.broadcasted_iota(jnp.int32, (2 * rows, width), 0) % 2
            ).astype(F32)
            spec[1] = nt_dot(fwd[...], lags[1]) + sign * spec[0]

    def send_own(t, carry):
        for d in range(2):
            ring_copy(d, 1, t).start()
        core_copy(0, t).start()
        return carry

    lax.fori_loop(0, CHUNKS, send_own, 0)

    @pl.when(seq == 0)
    def _():
        filter_copy().start()

    for hop in range(1, far + 1):

        def pair(p, carry, hop=hop):
            t = 2 * p + 1
            pass_on(hop, t - 1)
            pass_on(hop, t)
            project(hop - 1, t)
            if hop == far:
                project(far, t)
                finalize(t)
            return carry

        lax.fori_loop(0, CHUNKS // 2, pair, 0)
        if hop == 2:
            filter_spectra()

    @pl.when(seq == 1)
    def _():
        halo_copy().wait_recv()
        gate(0)

    first = lax.broadcasted_iota(jnp.int32, (rows, width), 0) == 0

    def term(lag, source):
        signal = jnp.dot(fwd[...], source[...], preferred_element_type=F32)
        return times(
            spec[lag, :rows], spec[lag, rows:], signal[:rows], signal[rows:], first
        )

    total[0], total[1] = term(0, gated)

    @pl.when(seq == 1)
    def _():
        for t in range(CHUNKS):
            gated_copy(t).wait_recv()
        real_part, imag_part = term(1, gated_in)
        total[0] += real_part
        total[1] += imag_part

    scale = jnp.where(first, 0.5, 1.0) / rows
    spectrum = jnp.concatenate(
        [(total[0] * scale).astype(BF16), (total[1] * scale).astype(BF16)], axis=0
    )
    conv = jnp.dot(inv[...], spectrum, preferred_element_type=F32)
    for t in range(CHUNKS):
        here = slice(t * size, (t + 1) * size)
        out[here, :] = (
            short(0, t) * (conv[here] + gain[...] * gated[here, :].astype(F32))
        ).astype(BF16)

    def finish(t, carry):
        for hop in range(1, far):
            for d in range(2):
                ring_copy(d, hop, t).wait_send()
        for d in range(2):

            @pl.when(t % 2 == d)
            def _(d=d):
                ring_copy(d, far, t).wait_send()

        for slot in range(last_slot + 1):
            core_copy(slot, t).wait_send()

        @pl.when(seq == 0)
        def _():
            gated_copy(t).wait_send()

        return carry

    lax.fori_loop(0, CHUNKS, finish, 0)

    @pl.when(seq == 0)
    def _():
        halo_copy().wait_send()
        filter_copy().wait_send()


def fused(chips, activations, in_weight, short_taps, long_filter, skip_gain):
    rows, depth = activations.shape
    width = in_weight.shape[1]
    forward, inverse = half_tables(rows)
    size = rows // CHUNKS
    here = pl.BlockSpec(memory_space=pltpu.VMEM)
    there = pl.BlockSpec(memory_space=pltpu.HBM)
    dma = pltpu.SemaphoreType.DMA
    return pl.pallas_call(
        functools.partial(fused_kernel, chips),
        out_shape=jax.ShapeDtypeStruct((rows, width), BF16),
        in_specs=[there] * 7,
        out_specs=here,
        scratch_shapes=[
            pltpu.VMEM((2, chips, CHUNKS, size, depth), BF16),
            pltpu.VMEM((2, chips, 3, width, depth), BF16),
            pltpu.VMEM((CHUNKS // 2, 3 * width, 2 * size), F32),
            pltpu.VMEM((3, rows + HALO, width), F32),
            pltpu.VMEM((rows, width), BF16),
            pltpu.VMEM((rows, width), BF16),
            pltpu.VMEM((2, width, rows), BF16),
            pltpu.VMEM((2 * rows, rows), BF16),
            pltpu.VMEM((rows, 2 * rows), BF16),
            pltpu.VMEM((3, 3, width), F32),
            pltpu.VMEM((1, width), F32),
            pltpu.VMEM((2, 2 * rows, width), F32),
            pltpu.VMEM((2, rows, width), F32),
            dma((chips, CHUNKS)),
            dma((chips, CHUNKS)),
            dma((chips, CHUNKS)),
            dma((chips, CHUNKS)),
            dma((CHUNKS,)),
            dma((2, chips)),
            dma((5,)),
            dma((CHUNKS + 2,)),
            dma((CHUNKS + 2,)),
        ],
        compiler_params=pltpu.CompilerParams(
            collective_id=0, has_side_effects=True, vmem_limit_bytes=63 * 1024 * 1024
        ),
        cost_estimate=pl.CostEstimate(
            flops=2 * rows * chips * 2 * depth * 3 * width,
            bytes_accessed=in_weight.size * 2,
            transcendentals=0,
        ),
    )(
        activations, in_weight, short_taps, long_filter, skip_gain[None, :],
        jnp.asarray(forward), jnp.asarray(inverse),
    )


def general(activations, in_weight, short_taps, long_filter, skip_gain):
    rows = activations.shape[0]
    channels = in_weight.shape[1]
    proj = jnp.einsum(
        "tk,sck->tsc",
        lax.all_gather(activations, "chan", axis=1, tiled=True),
        in_weight,
        preferred_element_type=F32,
    ).astype(BF16)
    earlier = from_behind(proj[rows - 2 :], "seq", 1)
    padded = jnp.concatenate([earlier, proj], axis=0).astype(F32)
    feat = (
        short_taps[:, 0, :] * padded[2:]
        + short_taps[:, 1, :] * padded[1:-1]
        + short_taps[:, 2, :] * padded[:-2]
    )
    gated = (feat[:, 1, :] * feat[:, 2, :]).astype(BF16)
    forward, inverse = (jnp.asarray(table) for table in half_tables(rows))
    seq_count = lax.axis_size("seq")
    all_lags = lax.all_gather(long_filter, "seq", axis=1, tiled=True)
    lag_blocks = all_lags.reshape(channels, seq_count, rows)
    spec = jnp.einsum("ft,cmt->mfc", forward, lag_blocks, preferred_element_type=F32)
    sign = (1.0 - 2.0 * (jnp.arange(2 * rows) % 2)).astype(F32)[:, None]
    spec = spec.at[1:].add(sign * spec[:-1])
    first = jnp.arange(rows)[:, None] == 0
    total = (jnp.zeros((rows, channels), F32), jnp.zeros((rows, channels), F32))
    moving = gated
    for section in range(seq_count):
        if section > 0:
            moving = from_behind(moving, "seq", 1)
        signal = jnp.dot(forward, moving, preferred_element_type=F32)
        part = times(
            spec[section, :rows], spec[section, rows:], signal[:rows], signal[rows:], first
        )
        total = (total[0] + part[0], total[1] + part[1])
    scale = jnp.where(first, 0.5, 1.0) / rows
    spectrum = jnp.concatenate([total[0] * scale, total[1] * scale], axis=0).astype(BF16)
    conv = jnp.dot(inverse, spectrum, preferred_element_type=F32)
    return (feat[:, 0, :] * (conv + skip_gain * gated.astype(F32))).astype(BF16)


def solution(mesh):
    in_specs = (
        P("seq", "chan"),
        P(None, "chan", None),
        P(None, None, "chan"),
        P("chan", "seq"),
        P("chan"),
    )
    out_specs = P("seq", "chan")
    chan = mesh.shape["chan"]
    if mesh.shape["seq"] == 2 and chan == 16:
        on_device = functools.partial(fused, chan // 2)
    else:
        on_device = general
    return jax.shard_map(
        on_device, mesh=mesh, in_specs=in_specs, out_specs=out_specs, check_vma=False
    )
```

```python
import functools
import math

import jax
import jax.numpy as jnp
import ml_dtypes
import numpy as np
from jax import lax
from jax.experimental import pallas as pl
from jax.experimental.pallas import tpu as pltpu
from jax.sharding import PartitionSpec as P

MESH = pl.DeviceIdType.MESH
F32 = jnp.float32
BF16 = jnp.bfloat16
CHUNKS = 4
HALO = 8


def from_behind(block, axis, distance):
    devices = range(lax.axis_size(axis))
    route = [(i - distance, i) for i in devices if i - distance in devices]
    return lax.ppermute(block, axis, route)


def half_tables(length):
    double = 2 * length
    index = np.arange(length, dtype=np.int64)
    phase = ((index[:, None] * index[None, :]) % double).astype(np.float32) * np.float32(
        2.0 * math.pi / double
    )
    cosine = np.cos(phase)
    sine = -np.sin(phase)
    sine[0] = 1.0 - 2.0 * (index % 2)
    forward = np.concatenate([cosine, sine], axis=0).astype(ml_dtypes.bfloat16)
    inverse = np.concatenate([cosine, sine.T], axis=1).astype(ml_dtypes.bfloat16)
    return forward, inverse


def times(fil_real, fil_imag, sig_real, sig_imag, first):
    cross = jnp.where(first, 0.0, fil_imag)
    real_part = fil_real * sig_real - cross * sig_imag
    imag_part = jnp.where(first, fil_imag, fil_real) * sig_imag + cross * sig_real
    return real_part, imag_part


def nt_dot(a, b):
    return lax.dot_general(a, b, (((1,), (1,)), ((), ())), preferred_element_type=F32)


def fused_kernel(
    chips, act, weight, taps_in, filt, gain_in, fwd_in, inv_in, out,
    blocks, wv, acc, proj, gated, gated_in, lags, fwd, inv, taps, gain, spec, total,
    ring_send, ring_recv, core_send, core_recv, own_sem, weight_sem, load_sem,
    seq_send, seq_recv,
):
    rows, depth = act.shape
    width = taps_in.shape[-1]
    size = rows // CHUNKS
    far = chips // 2
    full = far - 1
    last_slot = 2 * full + 1

    seq = lax.axis_index("seq")
    chan = lax.axis_index("chan")
    chip, core = chan // 2, chan % 2

    def chip_at(place):
        place = lax.rem(place + 2 * chips, chips)
        return jnp.where(place < far, 2 * place, 2 * (chips - 1 - place) + 1)

    place = jnp.where(chip % 2 == 0, chip // 2, chips - 1 - chip // 2)
    ahead = (chip_at(place + 1) * 2 + core, chip_at(place - 1) * 2 + core)
    sibling = chip * 2 + 1 - core

    def slot_of(d, hop):
        if hop == 0:
            return 0
        return last_slot if hop == far else 1 + d * full + hop - 1

    def slots_at(hop):
        return [slot_of(0, hop)] if hop in (0, far) else [slot_of(0, hop), slot_of(1, hop)]

    def chunk(t):
        return pl.ds(pl.multiple_of(t * size, size), size)

    def ring_copy(d, hop, t):
        src = blocks.at[0, slot_of(d, hop - 1), t]
        slot = slot_of(d, hop)
        return pltpu.make_async_remote_copy(
            src_ref=src, dst_ref=blocks.at[0, slot, t],
            send_sem=ring_send.at[slot, t], recv_sem=ring_recv.at[slot, t],
            device_id=(seq, ahead[d]), device_id_type=MESH,
        )

    def core_copy(slot, t):
        src = blocks.at[0, slot, t]
        return pltpu.make_async_remote_copy(
            src_ref=src, dst_ref=blocks.at[1, slot, t],
            send_sem=core_send.at[slot, t], recv_sem=core_recv.at[slot, t],
            device_id=(seq, sibling), device_id_type=MESH,
        )

    def seq_copy(src, dst, n):
        return pltpu.make_async_remote_copy(
            src_ref=src, dst_ref=dst, send_sem=seq_send.at[n], recv_sem=seq_recv.at[n],
            device_id=(1 - seq, chan), device_id_type=MESH,
        )

    def gated_copy(t):
        return seq_copy(gated.at[chunk(t)], gated_in.at[chunk(t)], t)

    def halo_copy():
        return seq_copy(proj.at[:, pl.ds(rows, HALO)], proj.at[:, pl.ds(0, HALO)], CHUNKS)

    def filter_copy():
        return seq_copy(filt, lags.at[0], CHUNKS + 1)

    def own_copy(t):
        return pltpu.make_async_copy(act.at[chunk(t)], blocks.at[0, 0, t], own_sem.at[t])

    def weight_copy(side, slot):
        if slot == 0:
            origin = chip
        elif slot == last_slot:
            origin = chip_at(place + far)
        elif slot <= full:
            origin = chip_at(place - slot)
        else:
            origin = chip_at(place + slot - full)
        block = origin * 2 + (core if side == 0 else 1 - core)
        cols = pl.ds(pl.multiple_of(block * depth, depth), depth)
        return pltpu.make_async_copy(
            weight.at[:, :, cols], wv.at[side, slot], weight_sem.at[side, slot]
        )

    fwd_copy = pltpu.make_async_copy(fwd_in, fwd, load_sem.at[0])
    inv_copy = pltpu.make_async_copy(inv_in, inv, load_sem.at[1])
    lag_copy = pltpu.make_async_copy(filt, lags.at[seq], load_sem.at[2])
    taps_copy = pltpu.make_async_copy(taps_in, taps, load_sem.at[3])
    gain_copy = pltpu.make_async_copy(gain_in, gain, load_sem.at[4])

    for t in range(CHUNKS):
        own_copy(t).start()
    barrier = pltpu.get_barrier_semaphore()
    for target in ((seq, ahead[0]), (seq, ahead[1]), (seq, sibling), (1 - seq, chan)):
        pl.semaphore_signal(barrier, inc=1, device_id=target, device_id_type=MESH)
    pl.semaphore_wait(barrier, 4)

    @pl.when(seq == 0)
    def _():
        proj[:, pl.ds(0, HALO), :] = jnp.zeros((3, HALO, width), F32)

    def short(stream, t):
        window = proj[stream, pl.ds(pl.multiple_of(t * size, size), size + HALO), :]
        return (
            taps[stream, 0, :][None] * window[HALO:]
            + taps[stream, 1, :][None] * window[HALO - 1 : HALO - 1 + size]
            + taps[stream, 2, :][None] * window[HALO - 2 : HALO - 2 + size]
        )

    def gate(t):
        gated[chunk(t), :] = (short(1, t) * short(2, t)).astype(BF16)

    def product(hop, t):
        parts = [(side, slot) for side in range(2) for slot in slots_at(hop)]

        @pl.when(t == 1)
        def _():
            for side, slot in parts:
                weight_copy(side, slot).wait()

        x = jnp.concatenate(
            [
                blocks[side, slot, pl.ds(t - 1, 2)].reshape(2 * size, depth)
                for side, slot in parts
            ],
            axis=1,
        )
        w = jnp.concatenate(
            [wv[side, slot].reshape(3 * width, depth) for side, slot in parts], axis=1
        )
        return nt_dot(w, x)

    def pass_on(hop, t):
        for d in range(2):
            if hop < far:
                ring_copy(d, hop, t).wait_recv()
                if hop < full:
                    ring_copy(d, hop + 1, t).start()
                else:

                    @pl.when(t % 2 == d)
                    def _(d=d):
                        ring_copy(d, far, t).start()

        if hop == far:
            ring_copy(0, far, t).wait_recv()
        for slot in slots_at(hop):
            core_copy(slot, t).start()

    def project(hop, t):
        for slot in slots_at(hop):
            core_copy(slot, t - 1).wait_recv()
            core_copy(slot, t).wait_recv()
        if hop == 0:
            acc[t // 2] = product(hop, t)
        else:
            acc[t // 2] += product(hop, t)

    def finalize(done):
        for stream in range(3):
            cols = slice(stream * width, (stream + 1) * width)
            start = pl.multiple_of((done - 1) * size + HALO, HALO)
            proj[stream, pl.ds(start, 2 * size), :] = (
                acc[done // 2, cols, :].astype(BF16).T.astype(F32)
            )

        @pl.when((seq == 0) & (done == CHUNKS - 1))
        def _():
            halo_copy().start()

        for t in (done - 1, done):

            @pl.when((seq == 0) | (t > 0))
            def _(t=t):
                gate(t)

            @pl.when(seq == 0)
            def _(t=t):
                gated_copy(t).start()

    def filter_spectra():
        fwd_copy.wait()
        inv_copy.wait()
        lag_copy.wait()
        taps_copy.wait()
        gain_copy.wait()

        @pl.when(seq == 1)
        def _():
            filter_copy().wait_recv()

        spec[0] = nt_dot(fwd[...], lags[0])

        @pl.when(seq == 1)
        def _():
            sign = 1.0 - 2.0 * (
                lax.broadcasted_iota(jnp.int32, (2 * rows, width), 0) % 2
            ).astype(F32)
            spec[1] = nt_dot(fwd[...], lags[1]) + sign * spec[0]

    def send_own(t, carry):
        own_copy(t).wait()
        for d in range(2):
            ring_copy(d, 1, t).start()
        core_copy(0, t).start()
        return carry

    lax.fori_loop(0, CHUNKS, send_own, 0)

    for hop in range(far + 1):
        for slot in slots_at(hop):
            for side in range(2):
                weight_copy(side, slot).start()
    lag_copy.start()
    fwd_copy.start()
    inv_copy.start()
    taps_copy.start()
    gain_copy.start()

    @pl.when(seq == 0)
    def _():
        filter_copy().start()

    for hop in range(1, far + 1):

        def pair(p, carry, hop=hop):
            t = 2 * p + 1
            pass_on(hop, t - 1)
            pass_on(hop, t)
            project(hop - 1, t)
            if hop == far:
                project(far, t)
                finalize(t)
            return carry

        lax.fori_loop(0, CHUNKS // 2, pair, 0)
        if hop == 2:
            filter_spectra()

    def finish(t, carry):
        for hop in range(1, far):
            for d in range(2):
                ring_copy(d, hop, t).wait_send()
        for d in range(2):

            @pl.when(t % 2 == d)
            def _(d=d):
                ring_copy(d, far, t).wait_send()

        for slot in range(last_slot + 1):
            core_copy(slot, t).wait_send()

        return carry

    lax.fori_loop(0, CHUNKS, finish, 0)

    @pl.when(seq == 1)
    def _():
        halo_copy().wait_recv()
        gate(0)

    first = lax.broadcasted_iota(jnp.int32, (rows, width), 0) == 0

    def term(lag, source):
        signal = jnp.dot(fwd[...], source[...], preferred_element_type=F32)
        return times(
            spec[lag, :rows], spec[lag, rows:], signal[:rows], signal[rows:], first
        )

    total[0], total[1] = term(0, gated)

    @pl.when(seq == 1)
    def _():
        for t in range(CHUNKS):
            gated_copy(t).wait_recv()
        real_part, imag_part = term(1, gated_in)
        total[0] += real_part
        total[1] += imag_part

    scale = jnp.where(first, 0.5, 1.0) / rows
    spectrum = jnp.concatenate(
        [(total[0] * scale).astype(BF16), (total[1] * scale).astype(BF16)], axis=0
    )
    conv = jnp.dot(inv[...], spectrum, preferred_element_type=F32)
    for t in range(CHUNKS):
        here = slice(t * size, (t + 1) * size)
        out[here, :] = (
            short(0, t) * (conv[here] + gain[...] * gated[here, :].astype(F32))
        ).astype(BF16)

    @pl.when(seq == 0)
    def _():
        for t in range(CHUNKS):
            gated_copy(t).wait_send()
        halo_copy().wait_send()
        filter_copy().wait_send()


def fused(chips, activations, in_weight, short_taps, long_filter, skip_gain):
    rows, depth = activations.shape
    width = in_weight.shape[1]
    forward, inverse = half_tables(rows)
    size = rows // CHUNKS
    here = pl.BlockSpec(memory_space=pltpu.VMEM)
    there = pl.BlockSpec(memory_space=pltpu.HBM)
    dma = pltpu.SemaphoreType.DMA
    return pl.pallas_call(
        functools.partial(fused_kernel, chips),
        out_shape=pltpu.VMEM((rows, width), BF16),
        in_specs=[there] * 7,
        out_specs=here,
        scratch_shapes=[
            pltpu.VMEM((2, chips, CHUNKS, size, depth), BF16),
            pltpu.VMEM((2, chips, 3, width, depth), BF16),
            pltpu.VMEM((CHUNKS // 2, 3 * width, 2 * size), F32),
            pltpu.VMEM((3, rows + HALO, width), F32),
            pltpu.VMEM((rows, width), BF16),
            pltpu.VMEM((rows, width), BF16),
            pltpu.VMEM((2, width, rows), BF16),
            pltpu.VMEM((2 * rows, rows), BF16),
            pltpu.VMEM((rows, 2 * rows), BF16),
            pltpu.VMEM((3, 3, width), F32),
            pltpu.VMEM((1, width), F32),
            pltpu.VMEM((2, 2 * rows, width), F32),
            pltpu.VMEM((2, rows, width), F32),
            dma((chips, CHUNKS)),
            dma((chips, CHUNKS)),
            dma((chips, CHUNKS)),
            dma((chips, CHUNKS)),
            dma((CHUNKS,)),
            dma((2, chips)),
            dma((5,)),
            dma((CHUNKS + 2,)),
            dma((CHUNKS + 2,)),
        ],
        compiler_params=pltpu.CompilerParams(
            collective_id=0, has_side_effects=True, vmem_limit_bytes=63 * 1024 * 1024
        ),
        cost_estimate=pl.CostEstimate(
            flops=2 * rows * chips * 2 * depth * 3 * width,
            bytes_accessed=in_weight.size * 2,
            transcendentals=0,
        ),
    )(
        activations, in_weight, short_taps, long_filter, skip_gain[None, :],
        jnp.asarray(forward), jnp.asarray(inverse),
    )


def general(activations, in_weight, short_taps, long_filter, skip_gain):
    rows = activations.shape[0]
    channels = in_weight.shape[1]
    proj = jnp.einsum(
        "tk,sck->tsc",
        lax.all_gather(activations, "chan", axis=1, tiled=True),
        in_weight,
        preferred_element_type=F32,
    ).astype(BF16)
    earlier = from_behind(proj[rows - 2 :], "seq", 1)
    padded = jnp.concatenate([earlier, proj], axis=0).astype(F32)
    feat = (
        short_taps[:, 0, :] * padded[2:]
        + short_taps[:, 1, :] * padded[1:-1]
        + short_taps[:, 2, :] * padded[:-2]
    )
    gated = (feat[:, 1, :] * feat[:, 2, :]).astype(BF16)
    forward, inverse = (jnp.asarray(table) for table in half_tables(rows))
    seq_count = lax.axis_size("seq")
    all_lags = lax.all_gather(long_filter, "seq", axis=1, tiled=True)
    lag_blocks = all_lags.reshape(channels, seq_count, rows)
    spec = jnp.einsum("ft,cmt->mfc", forward, lag_blocks, preferred_element_type=F32)
    sign = (1.0 - 2.0 * (jnp.arange(2 * rows) % 2)).astype(F32)[:, None]
    spec = spec.at[1:].add(sign * spec[:-1])
    first = jnp.arange(rows)[:, None] == 0
    total = (jnp.zeros((rows, channels), F32), jnp.zeros((rows, channels), F32))
    moving = gated
    for section in range(seq_count):
        if section > 0:
            moving = from_behind(moving, "seq", 1)
        signal = jnp.dot(forward, moving, preferred_element_type=F32)
        part = times(
            spec[section, :rows], spec[section, rows:], signal[:rows], signal[rows:], first
        )
        total = (total[0] + part[0], total[1] + part[1])
    scale = jnp.where(first, 0.5, 1.0) / rows
    spectrum = jnp.concatenate([total[0] * scale, total[1] * scale], axis=0).astype(BF16)
    conv = jnp.dot(inverse, spectrum, preferred_element_type=F32)
    return (feat[:, 0, :] * (conv + skip_gain * gated.astype(F32))).astype(BF16)


def solution(mesh):
    in_specs = (
        P("seq", "chan"),
        P(None, "chan", None),
        P(None, None, "chan"),
        P("chan", "seq"),
        P("chan"),
    )
    out_specs = P("seq", "chan")
    chan = mesh.shape["chan"]
    if mesh.shape["seq"] == 2 and chan == 16:
        on_device = functools.partial(fused, chan // 2)
    else:
        on_device = general
    return jax.shard_map(
        on_device, mesh=mesh, in_specs=in_specs, out_specs=out_specs, check_vma=False
    )
```

```python
import functools
import math

import jax
import jax.numpy as jnp
import ml_dtypes
import numpy as np
from jax import lax
from jax.experimental import pallas as pl
from jax.experimental.pallas import tpu as pltpu
from jax.sharding import PartitionSpec as P

MESH = pl.DeviceIdType.MESH
F32 = jnp.float32
BF16 = jnp.bfloat16
CHUNKS = 4
HALO = 8


def from_behind(block, axis, distance):
    devices = range(lax.axis_size(axis))
    route = [(i - distance, i) for i in devices if i - distance in devices]
    return lax.ppermute(block, axis, route)


def half_tables(length):
    double = 2 * length
    index = np.arange(length, dtype=np.int64)
    phase = ((index[:, None] * index[None, :]) % double).astype(np.float32) * np.float32(
        2.0 * math.pi / double
    )
    cosine = np.cos(phase)
    sine = -np.sin(phase)
    sine[0] = 1.0 - 2.0 * (index % 2)
    forward = np.concatenate([cosine, sine], axis=0).astype(ml_dtypes.bfloat16)
    inverse = np.concatenate([cosine, sine.T], axis=1).astype(ml_dtypes.bfloat16)
    return forward, inverse


def times(fil_real, fil_imag, sig_real, sig_imag, first):
    cross = jnp.where(first, 0.0, fil_imag)
    real_part = fil_real * sig_real - cross * sig_imag
    imag_part = jnp.where(first, fil_imag, fil_real) * sig_imag + cross * sig_real
    return real_part, imag_part


def nt_dot(a, b):
    return lax.dot_general(a, b, (((1,), (1,)), ((), ())), preferred_element_type=F32)


def fused_kernel(
    chips, act, weight, taps_in, filt, gain_in, fwd_in, inv_in, out,
    blocks, wv, acc, proj, gated, gated_in, lags, fwd, inv, taps, gain, spec, total,
    ring_send, ring_recv, core_send, core_recv, own_sem, weight_sem, load_sem,
    seq_send, seq_recv,
):
    rows, depth = act.shape
    width = taps_in.shape[-1]
    size = rows // CHUNKS
    far = chips // 2
    full = far - 1
    last_slot = 2 * full + 1

    seq = lax.axis_index("seq")
    chan = lax.axis_index("chan")
    chip, core = chan // 2, chan % 2

    def chip_at(place):
        place = lax.rem(place + 2 * chips, chips)
        return jnp.where(place < far, 2 * place, 2 * (chips - 1 - place) + 1)

    place = jnp.where(chip % 2 == 0, chip // 2, chips - 1 - chip // 2)
    ahead = (chip_at(place + 1) * 2 + core, chip_at(place - 1) * 2 + core)
    sibling = chip * 2 + 1 - core

    def slot_of(d, hop):
        if hop == 0:
            return 0
        return last_slot if hop == far else 1 + d * full + hop - 1

    def slots_at(hop):
        return [slot_of(0, hop)] if hop in (0, far) else [slot_of(0, hop), slot_of(1, hop)]

    def chunk(t):
        return pl.ds(pl.multiple_of(t * size, size), size)

    def ring_copy(d, hop, t):
        src = blocks.at[0, slot_of(d, hop - 1), t]
        slot = slot_of(d, hop)
        return pltpu.make_async_remote_copy(
            src_ref=src, dst_ref=blocks.at[0, slot, t],
            send_sem=ring_send.at[slot, t], recv_sem=ring_recv.at[slot, t],
            device_id=(seq, ahead[d]), device_id_type=MESH,
        )

    def core_copy(slot, t):
        src = blocks.at[0, slot, t]
        return pltpu.make_async_remote_copy(
            src_ref=src, dst_ref=blocks.at[1, slot, t],
            send_sem=core_send.at[slot, t], recv_sem=core_recv.at[slot, t],
            device_id=(seq, sibling), device_id_type=MESH,
        )

    def seq_copy(src, dst, n):
        return pltpu.make_async_remote_copy(
            src_ref=src, dst_ref=dst, send_sem=seq_send.at[n], recv_sem=seq_recv.at[n],
            device_id=(1 - seq, chan), device_id_type=MESH,
        )

    def gated_copy(t):
        return seq_copy(gated.at[chunk(t)], gated_in.at[chunk(t)], t)

    def halo_copy():
        return seq_copy(proj.at[:, pl.ds(rows, HALO)], proj.at[:, pl.ds(0, HALO)], CHUNKS)

    def filter_copy():
        return seq_copy(filt, lags.at[0], CHUNKS + 1)

    def own_copy(t):
        return pltpu.make_async_copy(act.at[chunk(t)], blocks.at[0, 0, t], own_sem.at[t])

    def weight_copy(side, slot):
        if slot == 0:
            origin = chip
        elif slot == last_slot:
            origin = chip_at(place + far)
        elif slot <= full:
            origin = chip_at(place - slot)
        else:
            origin = chip_at(place + slot - full)
        block = origin * 2 + (core if side == 0 else 1 - core)
        cols = pl.ds(pl.multiple_of(block * depth, depth), depth)
        return pltpu.make_async_copy(
            weight.at[:, :, cols], wv.at[side, slot], weight_sem.at[side, slot]
        )

    fwd_copy = pltpu.make_async_copy(fwd_in, fwd, load_sem.at[0])
    inv_copy = pltpu.make_async_copy(inv_in, inv, load_sem.at[1])
    lag_copy = pltpu.make_async_copy(filt, lags.at[seq], load_sem.at[2])
    taps_copy = pltpu.make_async_copy(taps_in, taps, load_sem.at[3])
    gain_copy = pltpu.make_async_copy(gain_in, gain, load_sem.at[4])

    for t in range(CHUNKS):
        own_copy(t).start()
    barrier = pltpu.get_barrier_semaphore()
    for target in ((seq, ahead[0]), (seq, ahead[1]), (seq, sibling), (1 - seq, chan)):
        pl.semaphore_signal(barrier, inc=1, device_id=target, device_id_type=MESH)
    pl.semaphore_wait(barrier, 4)

    @pl.when(seq == 0)
    def _():
        proj[:, pl.ds(0, HALO), :] = jnp.zeros((3, HALO, width), F32)

    def short(stream, t):
        window = proj[stream, pl.ds(pl.multiple_of(t * size, size), size + HALO), :]
        return (
            taps[stream, 0, :][None] * window[HALO:]
            + taps[stream, 1, :][None] * window[HALO - 1 : HALO - 1 + size]
            + taps[stream, 2, :][None] * window[HALO - 2 : HALO - 2 + size]
        )

    def gate(t):
        gated[chunk(t), :] = (short(1, t) * short(2, t)).astype(BF16)

    def product(hop, t):
        parts = [(side, slot) for side in range(2) for slot in slots_at(hop)]

        @pl.when(t == 1)
        def _():
            for side, slot in parts:
                weight_copy(side, slot).wait()

        x = jnp.concatenate(
            [
                blocks[side, slot, pl.ds(t - 1, 2)].reshape(2 * size, depth)
                for side, slot in parts
            ],
            axis=1,
        )
        w = jnp.concatenate(
            [wv[side, slot].reshape(3 * width, depth) for side, slot in parts], axis=1
        )
        return nt_dot(w, x)

    def send(d, hop, t):
        if hop == far:

            @pl.when(t % 2 == d)
            def _():
                ring_copy(d, full, CHUNKS - 2 + t // 2).wait_send()
                ring_copy(d, far, t).start()

        else:

            @pl.when(t >= 2)
            def _():
                ring_copy(d, hop, t - 2).wait_send()

            if hop > 1:

                @pl.when(t < 2)
                def _():
                    ring_copy(d, hop - 1, t + CHUNKS - 2).wait_send()

            ring_copy(d, hop, t).start()

    def pass_on(hop, t):
        if hop == far:
            ring_copy(0, far, t).wait_recv()
            core_copy(last_slot, t).start()
        else:
            for d in range(2):
                ring_copy(d, hop, t).wait_recv()
                core_copy(slot_of(d, hop), t).start()
                send(d, hop + 1, t)

    def project(hop, t):
        for slot in slots_at(hop):
            core_copy(slot, t - 1).wait_recv()
            core_copy(slot, t).wait_recv()
        if hop == 0:
            acc[t // 2] = product(hop, t)
        else:
            acc[t // 2] += product(hop, t)

    def finalize(done):
        for stream in range(3):
            cols = slice(stream * width, (stream + 1) * width)
            start = pl.multiple_of((done - 1) * size + HALO, HALO)
            proj[stream, pl.ds(start, 2 * size), :] = (
                acc[done // 2, cols, :].astype(BF16).T.astype(F32)
            )

        @pl.when((seq == 0) & (done == CHUNKS - 1))
        def _():
            halo_copy().start()

        for t in (done - 1, done):

            @pl.when((seq == 0) | (t > 0))
            def _(t=t):
                gate(t)

            @pl.when(seq == 0)
            def _(t=t):
                gated_copy(t).start()

    def filter_spectra():
        fwd_copy.wait()
        inv_copy.wait()
        lag_copy.wait()
        taps_copy.wait()
        gain_copy.wait()

        @pl.when(seq == 1)
        def _():
            filter_copy().wait_recv()

        spec[0] = nt_dot(fwd[...], lags[0])

        @pl.when(seq == 1)
        def _():
            sign = 1.0 - 2.0 * (
                lax.broadcasted_iota(jnp.int32, (2 * rows, width), 0) % 2
            ).astype(F32)
            spec[1] = nt_dot(fwd[...], lags[1]) + sign * spec[0]

    def send_own(t, carry):
        own_copy(t).wait()
        core_copy(0, t).start()
        for d in range(2):
            send(d, 1, t)
        return carry

    lax.fori_loop(0, 2, send_own, 0)

    for hop in range(far + 1):
        for slot in slots_at(hop):
            for side in range(2):
                weight_copy(side, slot).start()
    lag_copy.start()
    fwd_copy.start()
    inv_copy.start()
    taps_copy.start()
    gain_copy.start()

    @pl.when(seq == 0)
    def _():
        filter_copy().start()

    lax.fori_loop(2, CHUNKS, send_own, 0)

    for hop in range(1, far + 1):

        def pair(p, carry, hop=hop):
            t = 2 * p + 1
            pass_on(hop, t - 1)
            pass_on(hop, t)
            project(hop - 1, t)
            if hop == far:
                project(far, t)
                finalize(t)
            return carry

        lax.fori_loop(0, CHUNKS // 2, pair, 0)
        if hop == 2:
            filter_spectra()

    def finish(t, carry):
        for d in range(2):

            @pl.when(t % 2 == d)
            def _(d=d):
                ring_copy(d, far, t).wait_send()

        for slot in range(last_slot + 1):
            core_copy(slot, t).wait_send()

        return carry

    lax.fori_loop(0, CHUNKS, finish, 0)

    @pl.when(seq == 1)
    def _():
        halo_copy().wait_recv()
        gate(0)

    first = lax.broadcasted_iota(jnp.int32, (rows, width), 0) == 0

    def term(lag, source):
        signal = jnp.dot(fwd[...], source[...], preferred_element_type=F32)
        return times(
            spec[lag, :rows], spec[lag, rows:], signal[:rows], signal[rows:], first
        )

    total[0], total[1] = term(0, gated)

    @pl.when(seq == 1)
    def _():
        for t in range(CHUNKS):
            gated_copy(t).wait_recv()
        real_part, imag_part = term(1, gated_in)
        total[0] += real_part
        total[1] += imag_part

    scale = jnp.where(first, 0.5, 1.0) / rows
    spectrum = jnp.concatenate(
        [(total[0] * scale).astype(BF16), (total[1] * scale).astype(BF16)], axis=0
    )
    conv = jnp.dot(inv[...], spectrum, preferred_element_type=F32)
    for t in range(CHUNKS):
        here = slice(t * size, (t + 1) * size)
        out[here, :] = (
            short(0, t) * (conv[here] + gain[...] * gated[here, :].astype(F32))
        ).astype(BF16)

    @pl.when(seq == 0)
    def _():
        for t in range(CHUNKS):
            gated_copy(t).wait_send()
        halo_copy().wait_send()
        filter_copy().wait_send()


def fused(chips, activations, in_weight, short_taps, long_filter, skip_gain):
    rows, depth = activations.shape
    width = in_weight.shape[1]
    forward, inverse = half_tables(rows)
    size = rows // CHUNKS
    here = pl.BlockSpec(memory_space=pltpu.VMEM)
    there = pl.BlockSpec(memory_space=pltpu.HBM)
    dma = pltpu.SemaphoreType.DMA
    return pl.pallas_call(
        functools.partial(fused_kernel, chips),
        out_shape=pltpu.VMEM((rows, width), BF16),
        in_specs=[there] * 7,
        out_specs=here,
        scratch_shapes=[
            pltpu.VMEM((2, chips, CHUNKS, size, depth), BF16),
            pltpu.VMEM((2, chips, 3, width, depth), BF16),
            pltpu.VMEM((CHUNKS // 2, 3 * width, 2 * size), F32),
            pltpu.VMEM((3, rows + HALO, width), F32),
            pltpu.VMEM((rows, width), BF16),
            pltpu.VMEM((rows, width), BF16),
            pltpu.VMEM((2, width, rows), BF16),
            pltpu.VMEM((2 * rows, rows), BF16),
            pltpu.VMEM((rows, 2 * rows), BF16),
            pltpu.VMEM((3, 3, width), F32),
            pltpu.VMEM((1, width), F32),
            pltpu.VMEM((2, 2 * rows, width), F32),
            pltpu.VMEM((2, rows, width), F32),
            dma((chips, CHUNKS)),
            dma((chips, CHUNKS)),
            dma((chips, CHUNKS)),
            dma((chips, CHUNKS)),
            dma((CHUNKS,)),
            dma((2, chips)),
            dma((5,)),
            dma((CHUNKS + 2,)),
            dma((CHUNKS + 2,)),
        ],
        compiler_params=pltpu.CompilerParams(
            collective_id=0, has_side_effects=True, vmem_limit_bytes=63 * 1024 * 1024
        ),
        cost_estimate=pl.CostEstimate(
            flops=2 * rows * chips * 2 * depth * 3 * width,
            bytes_accessed=in_weight.size * 2,
            transcendentals=0,
        ),
    )(
        activations, in_weight, short_taps, long_filter, skip_gain[None, :],
        jnp.asarray(forward), jnp.asarray(inverse),
    )


def general(activations, in_weight, short_taps, long_filter, skip_gain):
    rows = activations.shape[0]
    channels = in_weight.shape[1]
    proj = jnp.einsum(
        "tk,sck->tsc",
        lax.all_gather(activations, "chan", axis=1, tiled=True),
        in_weight,
        preferred_element_type=F32,
    ).astype(BF16)
    earlier = from_behind(proj[rows - 2 :], "seq", 1)
    padded = jnp.concatenate([earlier, proj], axis=0).astype(F32)
    feat = (
        short_taps[:, 0, :] * padded[2:]
        + short_taps[:, 1, :] * padded[1:-1]
        + short_taps[:, 2, :] * padded[:-2]
    )
    gated = (feat[:, 1, :] * feat[:, 2, :]).astype(BF16)
    forward, inverse = (jnp.asarray(table) for table in half_tables(rows))
    seq_count = lax.axis_size("seq")
    all_lags = lax.all_gather(long_filter, "seq", axis=1, tiled=True)
    lag_blocks = all_lags.reshape(channels, seq_count, rows)
    spec = jnp.einsum("ft,cmt->mfc", forward, lag_blocks, preferred_element_type=F32)
    sign = (1.0 - 2.0 * (jnp.arange(2 * rows) % 2)).astype(F32)[:, None]
    spec = spec.at[1:].add(sign * spec[:-1])
    first = jnp.arange(rows)[:, None] == 0
    total = (jnp.zeros((rows, channels), F32), jnp.zeros((rows, channels), F32))
    moving = gated
    for section in range(seq_count):
        if section > 0:
            moving = from_behind(moving, "seq", 1)
        signal = jnp.dot(forward, moving, preferred_element_type=F32)
        part = times(
            spec[section, :rows], spec[section, rows:], signal[:rows], signal[rows:], first
        )
        total = (total[0] + part[0], total[1] + part[1])
    scale = jnp.where(first, 0.5, 1.0) / rows
    spectrum = jnp.concatenate([total[0] * scale, total[1] * scale], axis=0).astype(BF16)
    conv = jnp.dot(inverse, spectrum, preferred_element_type=F32)
    return (feat[:, 0, :] * (conv + skip_gain * gated.astype(F32))).astype(BF16)


def solution(mesh):
    in_specs = (
        P("seq", "chan"),
        P(None, "chan", None),
        P(None, None, "chan"),
        P("chan", "seq"),
        P("chan"),
    )
    out_specs = P("seq", "chan")
    chan = mesh.shape["chan"]
    if mesh.shape["seq"] == 2 and chan == 16:
        on_device = functools.partial(fused, chan // 2)
    else:
        on_device = general
    return jax.shard_map(
        on_device, mesh=mesh, in_specs=in_specs, out_specs=out_specs, check_vma=False
    )
```

```python
import functools
import math

import jax
import jax.numpy as jnp
import ml_dtypes
import numpy as np
from jax import lax
from jax.experimental import pallas as pl
from jax.experimental.pallas import tpu as pltpu
from jax.sharding import PartitionSpec as P

MESH = pl.DeviceIdType.MESH
F32 = jnp.float32
BF16 = jnp.bfloat16
CHUNKS = 4
HALO = 8
Q, KV, QKV = slice(0, 1), slice(1, 3), slice(0, 3)


def from_behind(block, axis, distance):
    devices = range(lax.axis_size(axis))
    route = [(i - distance, i) for i in devices if i - distance in devices]
    return lax.ppermute(block, axis, route)


def half_tables(length):
    double = 2 * length
    index = np.arange(length, dtype=np.int64)
    phase = ((index[:, None] * index[None, :]) % double).astype(np.float32) * np.float32(
        2.0 * math.pi / double
    )
    cosine = np.cos(phase)
    sine = -np.sin(phase)
    sine[0] = 1.0 - 2.0 * (index % 2)
    forward = np.concatenate([cosine, sine], axis=0).astype(ml_dtypes.bfloat16)
    inverse = np.concatenate([cosine, sine.T], axis=1).astype(ml_dtypes.bfloat16)
    return forward, inverse


def times(fil_real, fil_imag, sig_real, sig_imag, first):
    cross = jnp.where(first, 0.0, fil_imag)
    real_part = fil_real * sig_real - cross * sig_imag
    imag_part = jnp.where(first, fil_imag, fil_real) * sig_imag + cross * sig_real
    return real_part, imag_part


def nt_dot(a, b):
    return lax.dot_general(a, b, (((1,), (1,)), ((), ())), preferred_element_type=F32)


def fused_kernel(
    chips, act, weight, taps_in, filt, gain_in, fwd_in, inv_in, out,
    blocks, wv, acc, proj, gated, gated_in, lags, fwd, inv, taps, gain, spec, total, early,
    ring_send, ring_recv, core_send, core_recv, own_sem, weight_sem, load_sem,
    seq_send, seq_recv,
):
    rows, depth = act.shape
    width = taps_in.shape[-1]
    size = rows // CHUNKS
    far = chips // 2
    full = far - 1
    last_slot = 2 * full + 1

    seq = lax.axis_index("seq")
    chan = lax.axis_index("chan")
    chip, core = chan // 2, chan % 2

    def chip_at(place):
        place = lax.rem(place + 2 * chips, chips)
        return jnp.where(place < far, 2 * place, 2 * (chips - 1 - place) + 1)

    place = jnp.where(chip % 2 == 0, chip // 2, chips - 1 - chip // 2)
    ahead = (chip_at(place + 1) * 2 + core, chip_at(place - 1) * 2 + core)
    sibling = chip * 2 + 1 - core

    def slot_of(d, hop):
        if hop == 0:
            return 0
        return last_slot if hop == far else 1 + d * full + hop - 1

    def slots_at(hop):
        return [slot_of(0, hop)] if hop in (0, far) else [slot_of(0, hop), slot_of(1, hop)]

    def chunk(t):
        return pl.ds(pl.multiple_of(t * size, size), size)

    def ring_copy(d, hop, t):
        src = blocks.at[0, slot_of(d, hop - 1), t]
        slot = slot_of(d, hop)
        return pltpu.make_async_remote_copy(
            src_ref=src, dst_ref=blocks.at[0, slot, t],
            send_sem=ring_send.at[slot, t], recv_sem=ring_recv.at[slot, t],
            device_id=(seq, ahead[d]), device_id_type=MESH,
        )

    def core_copy(slot, t):
        src = blocks.at[0, slot, t]
        return pltpu.make_async_remote_copy(
            src_ref=src, dst_ref=blocks.at[1, slot, t],
            send_sem=core_send.at[slot, t], recv_sem=core_recv.at[slot, t],
            device_id=(seq, sibling), device_id_type=MESH,
        )

    def seq_copy(src, dst, n):
        return pltpu.make_async_remote_copy(
            src_ref=src, dst_ref=dst, send_sem=seq_send.at[n], recv_sem=seq_recv.at[n],
            device_id=(1 - seq, chan), device_id_type=MESH,
        )

    def gated_copy(t):
        return seq_copy(gated.at[chunk(t)], gated_in.at[chunk(t)], t)

    def halo_copy(streams):
        return seq_copy(
            proj.at[streams, pl.ds(rows, HALO)], proj.at[streams, pl.ds(0, HALO)],
            CHUNKS + (streams is Q),
        )

    def filter_copy():
        return seq_copy(filt, lags.at[0], CHUNKS + 2)

    def own_copy(t):
        return pltpu.make_async_copy(act.at[chunk(t)], blocks.at[0, 0, t], own_sem.at[t])

    def weight_copy(side, slot):
        if slot == 0:
            origin = chip
        elif slot == last_slot:
            origin = chip_at(place + far)
        elif slot <= full:
            origin = chip_at(place - slot)
        else:
            origin = chip_at(place + slot - full)
        block = origin * 2 + (core if side == 0 else 1 - core)
        cols = pl.ds(pl.multiple_of(block * depth, depth), depth)
        return pltpu.make_async_copy(
            weight.at[:, :, cols], wv.at[side, slot], weight_sem.at[side, slot]
        )

    fwd_copy = pltpu.make_async_copy(fwd_in, fwd, load_sem.at[0])
    inv_copy = pltpu.make_async_copy(inv_in, inv, load_sem.at[1])
    lag_copy = pltpu.make_async_copy(filt, lags.at[seq], load_sem.at[2])
    taps_copy = pltpu.make_async_copy(taps_in, taps, load_sem.at[3])
    gain_copy = pltpu.make_async_copy(gain_in, gain, load_sem.at[4])

    for t in range(CHUNKS):
        own_copy(t).start()
    barrier = pltpu.get_barrier_semaphore()
    for target in ((seq, ahead[0]), (seq, ahead[1]), (seq, sibling), (1 - seq, chan)):
        pl.semaphore_signal(barrier, inc=1, device_id=target, device_id_type=MESH)
    pl.semaphore_wait(barrier, 4)

    @pl.when(seq == 0)
    def _():
        proj[:, pl.ds(0, HALO), :] = jnp.zeros((3, HALO, width), F32)

    def short(stream, t):
        window = proj[stream, pl.ds(pl.multiple_of(t * size, size), size + HALO), :]
        return (
            taps[stream, 0, :][None] * window[HALO:]
            + taps[stream, 1, :][None] * window[HALO - 1 : HALO - 1 + size]
            + taps[stream, 2, :][None] * window[HALO - 2 : HALO - 2 + size]
        )

    def gate(t):
        gated[chunk(t), :] = (short(1, t) * short(2, t)).astype(BF16)

    def arrive(hop, d, t):
        ring_copy(d, hop, t).wait_recv()
        core_copy(slot_of(d, hop), t).start()

    def pass_on(hop, index):
        for d in range(2):
            t = index ^ d
            arrive(hop, d, t)
            if hop < full or index % 2 == 0:
                ring_copy(d, hop + 1, t).start()

    def arrive_far(p):
        for d in range(2):
            arrive(far, d, 2 * p + d)

    def project(hop, p, streams=QKV):
        parts = [(side, slot) for side in range(2) for slot in slots_at(hop)]
        if streams is not Q:
            for side, slot in parts:
                if p == 0:
                    weight_copy(side, slot).wait()
                if side == 1:
                    core_copy(slot, 2 * p).wait_recv()
                    core_copy(slot, 2 * p + 1).wait_recv()
        x = jnp.concatenate(
            [
                blocks[side, slot, pl.ds(2 * p, 2)].reshape(2 * size, depth)
                for side, slot in parts
            ],
            axis=1,
        )
        count = streams.stop - streams.start
        w = jnp.concatenate(
            [wv[side, slot, streams].reshape(count * width, depth) for side, slot in parts],
            axis=1,
        )
        here = slice(streams.start * width, streams.stop * width)
        if hop == 0:
            acc[p, here] = nt_dot(w, x)
        else:
            acc[p, here] += nt_dot(w, x)

    def round_up(p, streams):
        for stream in range(streams.start, streams.stop):
            cols = slice(stream * width, (stream + 1) * width)
            proj[stream, pl.ds(2 * p * size + HALO, 2 * size), :] = (
                acc[p, cols, :].astype(BF16).T.astype(F32)
            )

        if p == CHUNKS // 2 - 1:

            @pl.when(seq == 0)
            def _():
                halo_copy(streams).start()

    def gate_pair(p):
        for t in (2 * p, 2 * p + 1):
            if t > 0:
                gate(t)

                @pl.when(seq == 0)
                def _(t=t):
                    gated_copy(t).start()

            else:

                @pl.when(seq == 0)
                def _(t=t):
                    gate(t)
                    gated_copy(t).start()

    def filter_spectra():
        fwd_copy.wait()
        inv_copy.wait()
        lag_copy.wait()
        taps_copy.wait()
        gain_copy.wait()

        @pl.when(seq == 1)
        def _():
            filter_copy().wait_recv()

        spec[0] = nt_dot(fwd[...], lags[0])

        @pl.when(seq == 1)
        def _():
            sign = 1.0 - 2.0 * (
                lax.broadcasted_iota(jnp.int32, (2 * rows, width), 0) % 2
            ).astype(F32)
            spec[1] = nt_dot(fwd[...], lags[1]) + sign * spec[0]

    def send_own(p):
        for t in (2 * p, 2 * p + 1):
            own_copy(t).wait()
        for index in (2 * p, 2 * p + 1):
            for d in range(2):
                ring_copy(d, 1, index ^ d).start()
        for t in (2 * p, 2 * p + 1):
            core_copy(0, t).start()

    send_own(0)
    send_own(1)
    for hop in range(far + 1):
        for slot in slots_at(hop):
            for side in range(2):
                weight_copy(side, slot).start()
    lag_copy.start()
    fwd_copy.start()
    inv_copy.start()
    taps_copy.start()
    gain_copy.start()

    @pl.when(seq == 0)
    def _():
        filter_copy().start()

    pass_on(1, 0)
    pass_on(1, 1)
    project(0, 0)
    pass_on(1, 2)
    project(0, 1)
    pass_on(2, 0)
    pass_on(2, 1)
    project(1, 0)
    pass_on(1, 3)
    pass_on(3, 0)
    pass_on(3, 1)
    project(2, 0)
    pass_on(2, 2)
    project(1, 1)
    filter_spectra()
    pass_on(2, 3)
    project(3, 0)
    arrive_far(0)
    project(2, 1)
    pass_on(3, 2)
    project(4, 0)
    round_up(0, QKV)
    gate_pair(0)
    pass_on(3, 3)
    project(3, 1)
    arrive_far(1)
    project(4, 1, KV)
    round_up(1, KV)
    gate_pair(1)
    project(4, 1, Q)
    round_up(1, Q)

    def finish(t, carry):
        for hop in range(1, far):
            for d in range(2):
                ring_copy(d, hop, t).wait_send()
        for d in range(2):

            @pl.when(t % 2 == d)
            def _(d=d):
                ring_copy(d, far, t).wait_send()

        for slot in range(last_slot + 1):
            core_copy(slot, t).wait_send()

        return carry

    lax.fori_loop(0, CHUNKS, finish, 0)

    @pl.when(seq == 1)
    def _():
        halo_copy(KV).wait_recv()
        gate(0)

    first = lax.broadcasted_iota(jnp.int32, (rows, width), 0) == 0

    def term(lag, signal):
        return times(
            spec[lag, :rows], spec[lag, rows:], signal[:rows], signal[rows:], first
        )

    total[0], total[1] = term(
        0, jnp.dot(fwd[...], gated[...], preferred_element_type=F32)
    )

    @pl.when(seq == 1)
    def _():
        half = rows // 2
        for t in range(CHUNKS // 2):
            gated_copy(t).wait_recv()
        early[...] = jnp.dot(
            fwd[:, :half], gated_in[:half], preferred_element_type=F32
        )
        for t in range(CHUNKS // 2, CHUNKS):
            gated_copy(t).wait_recv()
        late = jnp.dot(fwd[:, half:], gated_in[half:], preferred_element_type=F32)
        real_part, imag_part = term(1, early[...] + late)
        halo_copy(Q).wait_recv()
        total[0] += real_part
        total[1] += imag_part

    scale = jnp.where(first, 0.5, 1.0) / rows
    spectrum = jnp.concatenate(
        [(total[0] * scale).astype(BF16), (total[1] * scale).astype(BF16)], axis=0
    )
    conv = jnp.dot(inv[...], spectrum, preferred_element_type=F32)
    for t in range(CHUNKS):
        here = slice(t * size, (t + 1) * size)
        out[here, :] = (
            short(0, t) * (conv[here] + gain[...] * gated[here, :].astype(F32))
        ).astype(BF16)

    @pl.when(seq == 0)
    def _():
        for t in range(CHUNKS):
            gated_copy(t).wait_send()
        halo_copy(KV).wait_send()
        halo_copy(Q).wait_send()
        filter_copy().wait_send()


def fused(chips, activations, in_weight, short_taps, long_filter, skip_gain):
    rows, depth = activations.shape
    width = in_weight.shape[1]
    forward, inverse = half_tables(rows)
    size = rows // CHUNKS
    here = pl.BlockSpec(memory_space=pltpu.VMEM)
    there = pl.BlockSpec(memory_space=pltpu.HBM)
    dma = pltpu.SemaphoreType.DMA
    return pl.pallas_call(
        functools.partial(fused_kernel, chips),
        out_shape=pltpu.VMEM((rows, width), BF16),
        in_specs=[there] * 7,
        out_specs=here,
        scratch_shapes=[
            pltpu.VMEM((2, chips, CHUNKS, size, depth), BF16),
            pltpu.VMEM((2, chips, 3, width, depth), BF16),
            pltpu.VMEM((CHUNKS // 2, 3 * width, 2 * size), F32),
            pltpu.VMEM((3, rows + HALO, width), F32),
            pltpu.VMEM((rows, width), BF16),
            pltpu.VMEM((rows, width), BF16),
            pltpu.VMEM((2, width, rows), BF16),
            pltpu.VMEM((2 * rows, rows), BF16),
            pltpu.VMEM((rows, 2 * rows), BF16),
            pltpu.VMEM((3, 3, width), F32),
            pltpu.VMEM((1, width), F32),
            pltpu.VMEM((2, 2 * rows, width), F32),
            pltpu.VMEM((2, rows, width), F32),
            pltpu.VMEM((2 * rows, width), F32),
            dma((chips, CHUNKS)),
            dma((chips, CHUNKS)),
            dma((chips, CHUNKS)),
            dma((chips, CHUNKS)),
            dma((CHUNKS,)),
            dma((2, chips)),
            dma((5,)),
            dma((CHUNKS + 3,)),
            dma((CHUNKS + 3,)),
        ],
        compiler_params=pltpu.CompilerParams(
            collective_id=0, has_side_effects=True, vmem_limit_bytes=63 * 1024 * 1024
        ),
        cost_estimate=pl.CostEstimate(
            flops=2 * rows * chips * 2 * depth * 3 * width,
            bytes_accessed=in_weight.size * 2,
            transcendentals=0,
        ),
    )(
        activations, in_weight, short_taps, long_filter, skip_gain[None, :],
        jnp.asarray(forward), jnp.asarray(inverse),
    )


def general(activations, in_weight, short_taps, long_filter, skip_gain):
    rows = activations.shape[0]
    channels = in_weight.shape[1]
    proj = jnp.einsum(
        "tk,sck->tsc",
        lax.all_gather(activations, "chan", axis=1, tiled=True),
        in_weight,
        preferred_element_type=F32,
    ).astype(BF16)
    earlier = from_behind(proj[rows - 2 :], "seq", 1)
    padded = jnp.concatenate([earlier, proj], axis=0).astype(F32)
    feat = (
        short_taps[:, 0, :] * padded[2:]
        + short_taps[:, 1, :] * padded[1:-1]
        + short_taps[:, 2, :] * padded[:-2]
    )
    gated = (feat[:, 1, :] * feat[:, 2, :]).astype(BF16)
    forward, inverse = (jnp.asarray(table) for table in half_tables(rows))
    seq_count = lax.axis_size("seq")
    all_lags = lax.all_gather(long_filter, "seq", axis=1, tiled=True)
    lag_blocks = all_lags.reshape(channels, seq_count, rows)
    spec = jnp.einsum("ft,cmt->mfc", forward, lag_blocks, preferred_element_type=F32)
    sign = (1.0 - 2.0 * (jnp.arange(2 * rows) % 2)).astype(F32)[:, None]
    spec = spec.at[1:].add(sign * spec[:-1])
    first = jnp.arange(rows)[:, None] == 0
    total = (jnp.zeros((rows, channels), F32), jnp.zeros((rows, channels), F32))
    moving = gated
    for section in range(seq_count):
        if section > 0:
            moving = from_behind(moving, "seq", 1)
        signal = jnp.dot(forward, moving, preferred_element_type=F32)
        part = times(
            spec[section, :rows], spec[section, rows:], signal[:rows], signal[rows:], first
        )
        total = (total[0] + part[0], total[1] + part[1])
    scale = jnp.where(first, 0.5, 1.0) / rows
    spectrum = jnp.concatenate([total[0] * scale, total[1] * scale], axis=0).astype(BF16)
    conv = jnp.dot(inverse, spectrum, preferred_element_type=F32)
    return (feat[:, 0, :] * (conv + skip_gain * gated.astype(F32))).astype(BF16)


def solution(mesh):
    in_specs = (
        P("seq", "chan"),
        P(None, "chan", None),
        P(None, None, "chan"),
        P("chan", "seq"),
        P("chan"),
    )
    out_specs = P("seq", "chan")
    chan = mesh.shape["chan"]
    if mesh.shape["seq"] == 2 and chan == 16:
        on_device = functools.partial(fused, chan // 2)
    else:
        on_device = general
    return jax.shard_map(
        on_device, mesh=mesh, in_specs=in_specs, out_specs=out_specs, check_vma=False
    )
```

```python
import functools
import math

import jax
import jax.numpy as jnp
import ml_dtypes
import numpy as np
from jax import lax
from jax.experimental import pallas as pl
from jax.experimental.pallas import tpu as pltpu
from jax.sharding import PartitionSpec as P

MESH = pl.DeviceIdType.MESH
F32 = jnp.float32
BF16 = jnp.bfloat16
CHUNKS = 2
HALO = 8


def from_behind(block, axis, distance):
    devices = range(lax.axis_size(axis))
    route = [(i - distance, i) for i in devices if i - distance in devices]
    return lax.ppermute(block, axis, route)


def half_tables(length):
    double = 2 * length
    index = np.arange(length, dtype=np.int64)
    phase = ((index[:, None] * index[None, :]) % double).astype(np.float32) * np.float32(
        2.0 * math.pi / double
    )
    cosine = np.cos(phase)
    sine = -np.sin(phase)
    sine[0] = 1.0 - 2.0 * (index % 2)
    forward = np.concatenate([cosine, sine], axis=0).astype(ml_dtypes.bfloat16)
    inverse = np.concatenate([cosine, sine.T], axis=1).astype(ml_dtypes.bfloat16)
    return forward, inverse


def times(fil_real, fil_imag, sig_real, sig_imag, first):
    cross = jnp.where(first, 0.0, fil_imag)
    real_part = fil_real * sig_real - cross * sig_imag
    imag_part = jnp.where(first, fil_imag, fil_real) * sig_imag + cross * sig_real
    return real_part, imag_part


def nt_dot(a, b):
    return lax.dot_general(a, b, (((1,), (1,)), ((), ())), preferred_element_type=F32)


def fused_kernel(
    chips, act, weight, taps_in, filt, gain_in, fwd_in, inv_in, out,
    blocks, wv, acc, proj, gated, gated_in, lags, fwd, inv, taps, gain, spec, total,
    ring_send, ring_recv, core_send, core_recv, own_sem, weight_sem, load_sem,
    seq_send, seq_recv,
):
    rows, depth = act.shape
    width = taps_in.shape[-1]
    size = rows // CHUNKS
    far = chips // 2
    full = far - 1
    last_slot = 2 * full + 1

    seq = lax.axis_index("seq")
    chan = lax.axis_index("chan")
    chip, core = chan // 2, chan % 2

    def chip_at(place):
        place = lax.rem(place + 2 * chips, chips)
        return jnp.where(place < far, 2 * place, 2 * (chips - 1 - place) + 1)

    place = jnp.where(chip % 2 == 0, chip // 2, chips - 1 - chip // 2)
    ahead = (chip_at(place + 1) * 2 + core, chip_at(place - 1) * 2 + core)
    sibling = chip * 2 + 1 - core

    def slot_of(d, hop):
        if hop == 0:
            return 0
        return last_slot if hop == far else 1 + d * full + hop - 1

    def slots_at(hop):
        return [slot_of(0, hop)] if hop in (0, far) else [slot_of(0, hop), slot_of(1, hop)]

    def chunk(t):
        return pl.ds(pl.multiple_of(t * size, size), size)

    def ring_copy(d, hop, t):
        src = blocks.at[0, slot_of(d, hop - 1), t]
        slot = slot_of(d, hop)
        return pltpu.make_async_remote_copy(
            src_ref=src, dst_ref=blocks.at[0, slot, t],
            send_sem=ring_send.at[slot, t], recv_sem=ring_recv.at[slot, t],
            device_id=(seq, ahead[d]), device_id_type=MESH,
        )

    def core_copy(slot, t):
        src = blocks.at[0, slot, t]
        return pltpu.make_async_remote_copy(
            src_ref=src, dst_ref=blocks.at[1, slot, t],
            send_sem=core_send.at[slot, t], recv_sem=core_recv.at[slot, t],
            device_id=(seq, sibling), device_id_type=MESH,
        )

    def seq_copy(src, dst, n):
        return pltpu.make_async_remote_copy(
            src_ref=src, dst_ref=dst, send_sem=seq_send.at[n], recv_sem=seq_recv.at[n],
            device_id=(1 - seq, chan), device_id_type=MESH,
        )

    def gated_copy(t):
        return seq_copy(gated.at[chunk(t)], gated_in.at[chunk(t)], t)

    def halo_copy():
        return seq_copy(proj.at[:, pl.ds(rows, HALO)], proj.at[:, pl.ds(0, HALO)], CHUNKS)

    def filter_copy():
        return seq_copy(filt, lags.at[0], CHUNKS + 1)

    def own_copy(t):
        return pltpu.make_async_copy(act.at[chunk(t)], blocks.at[0, 0, t], own_sem.at[t])

    def weight_copy(side, slot):
        if slot == 0:
            origin = chip
        elif slot == last_slot:
            origin = chip_at(place + far)
        elif slot <= full:
            origin = chip_at(place - slot)
        else:
            origin = chip_at(place + slot - full)
        block = origin * 2 + (core if side == 0 else 1 - core)
        cols = pl.ds(pl.multiple_of(block * depth, depth), depth)
        return pltpu.make_async_copy(
            weight.at[:, :, cols], wv.at[side, slot], weight_sem.at[side, slot]
        )

    fwd_copy = pltpu.make_async_copy(fwd_in, fwd, load_sem.at[0])
    inv_copy = pltpu.make_async_copy(inv_in, inv, load_sem.at[1])
    lag_copy = pltpu.make_async_copy(filt, lags.at[seq], load_sem.at[2])
    taps_copy = pltpu.make_async_copy(taps_in, taps, load_sem.at[3])
    gain_copy = pltpu.make_async_copy(gain_in, gain, load_sem.at[4])

    for t in range(CHUNKS):
        own_copy(t).start()
    barrier = pltpu.get_barrier_semaphore()
    for target in ((seq, ahead[0]), (seq, ahead[1]), (seq, sibling), (1 - seq, chan)):
        pl.semaphore_signal(barrier, inc=1, device_id=target, device_id_type=MESH)
    pl.semaphore_wait(barrier, 4)

    @pl.when(seq == 0)
    def _():
        proj[:, pl.ds(0, HALO), :] = jnp.zeros((3, HALO, width), F32)

    def short(stream, t):
        window = proj[stream, pl.ds(pl.multiple_of(t * size, size), size + HALO), :]
        return (
            taps[stream, 0, :][None] * window[HALO:]
            + taps[stream, 1, :][None] * window[HALO - 1 : HALO - 1 + size]
            + taps[stream, 2, :][None] * window[HALO - 2 : HALO - 2 + size]
        )

    def gate(t):
        gated[chunk(t), :] = (short(1, t) * short(2, t)).astype(BF16)

    def product(hop, t):
        parts = [(side, slot) for side in range(2) for slot in slots_at(hop)]

        @pl.when(t == 1)
        def _():
            for side, slot in parts:
                weight_copy(side, slot).wait()

        x = jnp.concatenate(
            [
                blocks[side, slot, pl.ds(t - 1, 2)].reshape(2 * size, depth)
                for side, slot in parts
            ],
            axis=1,
        )
        w = jnp.concatenate(
            [wv[side, slot].reshape(3 * width, depth) for side, slot in parts], axis=1
        )
        return nt_dot(w, x)

    def pass_on(hop, t):
        for d in range(2):
            if hop < far:
                ring_copy(d, hop, t).wait_recv()
                if hop < full:
                    ring_copy(d, hop + 1, t).start()
                else:

                    @pl.when(t % 2 == d)
                    def _(d=d):
                        ring_copy(d, far, t).start()

        if hop == far:
            ring_copy(0, far, t).wait_recv()
        for slot in slots_at(hop):
            core_copy(slot, t).start()

    def project(hop, t):
        for slot in slots_at(hop):
            core_copy(slot, t - 1).wait_recv()
            core_copy(slot, t).wait_recv()
        if hop == 0:
            acc[t // 2] = product(hop, t)
        else:
            acc[t // 2] += product(hop, t)

    def finalize(done):
        for stream in range(3):
            cols = slice(stream * width, (stream + 1) * width)
            start = pl.multiple_of((done - 1) * size + HALO, HALO)
            proj[stream, pl.ds(start, 2 * size), :] = (
                acc[done // 2, cols, :].astype(BF16).T.astype(F32)
            )

        @pl.when((seq == 0) & (done == CHUNKS - 1))
        def _():
            halo_copy().start()

        for t in (done - 1, done):

            @pl.when((seq == 0) | (t > 0))
            def _(t=t):
                gate(t)

            @pl.when(seq == 0)
            def _(t=t):
                gated_copy(t).start()

    def filter_spectra():
        fwd_copy.wait()
        inv_copy.wait()
        lag_copy.wait()
        taps_copy.wait()
        gain_copy.wait()

        @pl.when(seq == 1)
        def _():
            filter_copy().wait_recv()

        spec[0] = nt_dot(fwd[...], lags[0])

        @pl.when(seq == 1)
        def _():
            sign = 1.0 - 2.0 * (
                lax.broadcasted_iota(jnp.int32, (2 * rows, width), 0) % 2
            ).astype(F32)
            spec[1] = nt_dot(fwd[...], lags[1]) + sign * spec[0]

    def send_own(t, carry):
        own_copy(t).wait()
        for d in range(2):
            ring_copy(d, 1, t).start()
        core_copy(0, t).start()
        return carry

    lax.fori_loop(0, CHUNKS, send_own, 0)

    for hop in range(far + 1):
        for slot in slots_at(hop):
            for side in range(2):
                weight_copy(side, slot).start()
    lag_copy.start()
    fwd_copy.start()
    inv_copy.start()
    taps_copy.start()
    gain_copy.start()

    @pl.when(seq == 0)
    def _():
        filter_copy().start()

    for hop in range(1, far + 1):

        def pair(p, carry, hop=hop):
            t = 2 * p + 1
            pass_on(hop, t - 1)
            pass_on(hop, t)
            project(hop - 1, t)
            if hop == far:
                project(far, t)
                finalize(t)
            return carry

        lax.fori_loop(0, CHUNKS // 2, pair, 0)
        if hop == 2:
            filter_spectra()

    def finish(t, carry):
        for hop in range(1, far):
            for d in range(2):
                ring_copy(d, hop, t).wait_send()
        for d in range(2):

            @pl.when(t % 2 == d)
            def _(d=d):
                ring_copy(d, far, t).wait_send()

        for slot in range(last_slot + 1):
            core_copy(slot, t).wait_send()

        return carry

    lax.fori_loop(0, CHUNKS, finish, 0)

    @pl.when(seq == 1)
    def _():
        halo_copy().wait_recv()
        gate(0)

    first = lax.broadcasted_iota(jnp.int32, (rows, width), 0) == 0

    def term(lag, source):
        signal = jnp.dot(fwd[...], source[...], preferred_element_type=F32)
        return times(
            spec[lag, :rows], spec[lag, rows:], signal[:rows], signal[rows:], first
        )

    total[0], total[1] = term(0, gated)

    @pl.when(seq == 1)
    def _():
        for t in range(CHUNKS):
            gated_copy(t).wait_recv()
        real_part, imag_part = term(1, gated_in)
        total[0] += real_part
        total[1] += imag_part

    scale = jnp.where(first, 0.5, 1.0) / rows
    spectrum = jnp.concatenate(
        [(total[0] * scale).astype(BF16), (total[1] * scale).astype(BF16)], axis=0
    )
    conv = jnp.dot(inv[...], spectrum, preferred_element_type=F32)
    for t in range(CHUNKS):
        here = slice(t * size, (t + 1) * size)
        out[here, :] = (
            short(0, t) * (conv[here] + gain[...] * gated[here, :].astype(F32))
        ).astype(BF16)

    @pl.when(seq == 0)
    def _():
        for t in range(CHUNKS):
            gated_copy(t).wait_send()
        halo_copy().wait_send()
        filter_copy().wait_send()


def fused(chips, activations, in_weight, short_taps, long_filter, skip_gain):
    rows, depth = activations.shape
    width = in_weight.shape[1]
    forward, inverse = half_tables(rows)
    size = rows // CHUNKS
    here = pl.BlockSpec(memory_space=pltpu.VMEM)
    there = pl.BlockSpec(memory_space=pltpu.HBM)
    dma = pltpu.SemaphoreType.DMA
    return pl.pallas_call(
        functools.partial(fused_kernel, chips),
        out_shape=pltpu.VMEM((rows, width), BF16),
        in_specs=[there] * 7,
        out_specs=here,
        scratch_shapes=[
            pltpu.VMEM((2, chips, CHUNKS, size, depth), BF16),
            pltpu.VMEM((2, chips, 3, width, depth), BF16),
            pltpu.VMEM((CHUNKS // 2, 3 * width, 2 * size), F32),
            pltpu.VMEM((3, rows + HALO, width), F32),
            pltpu.VMEM((rows, width), BF16),
            pltpu.VMEM((rows, width), BF16),
            pltpu.VMEM((2, width, rows), BF16),
            pltpu.VMEM((2 * rows, rows), BF16),
            pltpu.VMEM((rows, 2 * rows), BF16),
            pltpu.VMEM((3, 3, width), F32),
            pltpu.VMEM((1, width), F32),
            pltpu.VMEM((2, 2 * rows, width), F32),
            pltpu.VMEM((2, rows, width), F32),
            dma((chips, CHUNKS)),
            dma((chips, CHUNKS)),
            dma((chips, CHUNKS)),
            dma((chips, CHUNKS)),
            dma((CHUNKS,)),
            dma((2, chips)),
            dma((5,)),
            dma((CHUNKS + 2,)),
            dma((CHUNKS + 2,)),
        ],
        compiler_params=pltpu.CompilerParams(
            collective_id=0, has_side_effects=True, vmem_limit_bytes=63 * 1024 * 1024
        ),
        cost_estimate=pl.CostEstimate(
            flops=2 * rows * chips * 2 * depth * 3 * width,
            bytes_accessed=in_weight.size * 2,
            transcendentals=0,
        ),
    )(
        activations, in_weight, short_taps, long_filter, skip_gain[None, :],
        jnp.asarray(forward), jnp.asarray(inverse),
    )


def general(activations, in_weight, short_taps, long_filter, skip_gain):
    rows = activations.shape[0]
    channels = in_weight.shape[1]
    proj = jnp.einsum(
        "tk,sck->tsc",
        lax.all_gather(activations, "chan", axis=1, tiled=True),
        in_weight,
        preferred_element_type=F32,
    ).astype(BF16)
    earlier = from_behind(proj[rows - 2 :], "seq", 1)
    padded = jnp.concatenate([earlier, proj], axis=0).astype(F32)
    feat = (
        short_taps[:, 0, :] * padded[2:]
        + short_taps[:, 1, :] * padded[1:-1]
        + short_taps[:, 2, :] * padded[:-2]
    )
    gated = (feat[:, 1, :] * feat[:, 2, :]).astype(BF16)
    forward, inverse = (jnp.asarray(table) for table in half_tables(rows))
    seq_count = lax.axis_size("seq")
    all_lags = lax.all_gather(long_filter, "seq", axis=1, tiled=True)
    lag_blocks = all_lags.reshape(channels, seq_count, rows)
    spec = jnp.einsum("ft,cmt->mfc", forward, lag_blocks, preferred_element_type=F32)
    sign = (1.0 - 2.0 * (jnp.arange(2 * rows) % 2)).astype(F32)[:, None]
    spec = spec.at[1:].add(sign * spec[:-1])
    first = jnp.arange(rows)[:, None] == 0
    total = (jnp.zeros((rows, channels), F32), jnp.zeros((rows, channels), F32))
    moving = gated
    for section in range(seq_count):
        if section > 0:
            moving = from_behind(moving, "seq", 1)
        signal = jnp.dot(forward, moving, preferred_element_type=F32)
        part = times(
            spec[section, :rows], spec[section, rows:], signal[:rows], signal[rows:], first
        )
        total = (total[0] + part[0], total[1] + part[1])
    scale = jnp.where(first, 0.5, 1.0) / rows
    spectrum = jnp.concatenate([total[0] * scale, total[1] * scale], axis=0).astype(BF16)
    conv = jnp.dot(inverse, spectrum, preferred_element_type=F32)
    return (feat[:, 0, :] * (conv + skip_gain * gated.astype(F32))).astype(BF16)


def solution(mesh):
    in_specs = (
        P("seq", "chan"),
        P(None, "chan", None),
        P(None, None, "chan"),
        P("chan", "seq"),
        P("chan"),
    )
    out_specs = P("seq", "chan")
    chan = mesh.shape["chan"]
    if mesh.shape["seq"] == 2 and chan == 16:
        on_device = functools.partial(fused, chan // 2)
    else:
        on_device = general
    return jax.shard_map(
        on_device, mesh=mesh, in_specs=in_specs, out_specs=out_specs, check_vma=False
    )
```

```python
import functools
import math

import jax
import jax.numpy as jnp
import ml_dtypes
import numpy as np
from jax import lax
from jax.experimental import pallas as pl
from jax.experimental.pallas import tpu as pltpu
from jax.sharding import PartitionSpec as P

MESH = pl.DeviceIdType.MESH
F32 = jnp.float32
BF16 = jnp.bfloat16
CHUNKS = 4
HALO = 8


def from_behind(block, axis, distance):
    devices = range(lax.axis_size(axis))
    route = [(i - distance, i) for i in devices if i - distance in devices]
    return lax.ppermute(block, axis, route)


def half_tables(length):
    double = 2 * length
    index = np.arange(length, dtype=np.int64)
    phase = ((index[:, None] * index[None, :]) % double).astype(np.float32) * np.float32(
        2.0 * math.pi / double
    )
    cosine = np.cos(phase)
    sine = -np.sin(phase)
    sine[0] = 1.0 - 2.0 * (index % 2)
    forward = np.concatenate([cosine, sine], axis=0).astype(ml_dtypes.bfloat16)
    inverse = np.concatenate([cosine, sine.T], axis=1).astype(ml_dtypes.bfloat16)
    return forward, inverse


def times(fil_real, fil_imag, sig_real, sig_imag, first):
    cross = jnp.where(first, 0.0, fil_imag)
    real_part = fil_real * sig_real - cross * sig_imag
    imag_part = jnp.where(first, fil_imag, fil_real) * sig_imag + cross * sig_real
    return real_part, imag_part


def nt_dot(a, b):
    return lax.dot_general(a, b, (((1,), (1,)), ((), ())), preferred_element_type=F32)


def fused_kernel(
    chips, act, weight, taps_in, filt, gain_in, fwd_in, inv_in, out,
    blocks, wv, acc, proj, gated, lags, fwd, inv, taps, gain, spec, total,
    ring_send, ring_recv, core_send, core_recv, own_sem, weight_sem, load_sem,
    seq_send, seq_recv,
):
    rows, depth = act.shape
    width = taps_in.shape[-1]
    size = rows // CHUNKS
    far = chips // 2
    full = far - 1
    last_slot = 2 * full + 1

    seq = lax.axis_index("seq")
    chan = lax.axis_index("chan")
    chip, core = chan // 2, chan % 2

    def chip_at(place):
        place = lax.rem(place + 2 * chips, chips)
        return jnp.where(place < far, 2 * place, 2 * (chips - 1 - place) + 1)

    place = jnp.where(chip % 2 == 0, chip // 2, chips - 1 - chip // 2)
    ahead = (chip_at(place + 1) * 2 + core, chip_at(place - 1) * 2 + core)
    sibling = chip * 2 + 1 - core

    def slot_of(d, hop):
        if isinstance(hop, int):
            if hop == 0:
                return 0
            return last_slot if hop == far else d * full + hop
        return jnp.where(hop == 0, 0, jnp.where(hop == far, last_slot, d * full + hop))

    def slots_at(hop):
        return [slot_of(0, hop)] if hop in (0, far) else [slot_of(0, hop), slot_of(1, hop)]

    def chunk(t):
        return pl.ds(pl.multiple_of(t * size, size), size)

    def ring_copy(d, hop, t):
        src = blocks.at[0, slot_of(d, hop - 1), t]
        slot = slot_of(d, hop)
        return pltpu.make_async_remote_copy(
            src_ref=src, dst_ref=blocks.at[0, slot, t],
            send_sem=ring_send.at[slot, t], recv_sem=ring_recv.at[slot, t],
            device_id=(seq, ahead[d]), device_id_type=MESH,
        )

    def core_copy(slot, t):
        src = blocks.at[0, slot, t]
        return pltpu.make_async_remote_copy(
            src_ref=src, dst_ref=blocks.at[1, slot, t],
            send_sem=core_send.at[slot, t], recv_sem=core_recv.at[slot, t],
            device_id=(seq, sibling), device_id_type=MESH,
        )

    def seq_copy(src, dst, n):
        return pltpu.make_async_remote_copy(
            src_ref=src, dst_ref=dst, send_sem=seq_send.at[n], recv_sem=seq_recv.at[n],
            device_id=(1 - seq, chan), device_id_type=MESH,
        )

    def gated_copy(t):
        return seq_copy(gated.at[0, chunk(t)], gated.at[1, chunk(t)], t)

    def halo_copy():
        return seq_copy(proj.at[:, pl.ds(rows, HALO)], proj.at[:, pl.ds(0, HALO)], CHUNKS)

    def filter_copy():
        return seq_copy(filt, lags.at[0], CHUNKS + 1)

    def own_copy(t):
        return pltpu.make_async_copy(act.at[chunk(t)], blocks.at[0, 0, t], own_sem.at[t])

    def weight_copy(side, slot):
        if slot == 0:
            origin = chip
        elif slot == last_slot:
            origin = chip_at(place + far)
        elif slot <= full:
            origin = chip_at(place - slot)
        else:
            origin = chip_at(place + slot - full)
        block = origin * 2 + (core if side == 0 else 1 - core)
        cols = pl.ds(pl.multiple_of(block * depth, depth), depth)
        return pltpu.make_async_copy(
            weight.at[:, :, cols], wv.at[side, slot], weight_sem.at[side, slot]
        )

    fwd_copy = pltpu.make_async_copy(fwd_in, fwd, load_sem.at[0])
    inv_copy = pltpu.make_async_copy(inv_in, inv, load_sem.at[1])
    lag_copy = pltpu.make_async_copy(filt, lags.at[seq], load_sem.at[2])
    taps_copy = pltpu.make_async_copy(taps_in, taps, load_sem.at[3])
    gain_copy = pltpu.make_async_copy(gain_in, gain, load_sem.at[4])

    for t in range(CHUNKS):
        own_copy(t).start()
    barrier = pltpu.get_barrier_semaphore()
    for target in ((seq, ahead[0]), (seq, ahead[1]), (seq, sibling), (1 - seq, chan)):
        pl.semaphore_signal(barrier, inc=1, device_id=target, device_id_type=MESH)
    pl.semaphore_wait(barrier, 4)

    @pl.when(seq == 0)
    def _():
        proj[:, pl.ds(0, HALO), :] = jnp.zeros((3, HALO, width), F32)

    def short(stream, t):
        window = proj[stream, pl.ds(pl.multiple_of(t * size, size), size + HALO), :]
        return (
            taps[stream, 0, :][None] * window[HALO:]
            + taps[stream, 1, :][None] * window[HALO - 1 : HALO - 1 + size]
            + taps[stream, 2, :][None] * window[HALO - 2 : HALO - 2 + size]
        )

    def gate(t):
        gated[0, chunk(t), :] = (short(1, t) * short(2, t)).astype(BF16)

    def pass_on(hop, t):
        for d in range(2):

            @pl.when(hop < far)
            def _(d=d):
                ring_copy(d, hop, t).wait_recv()

            @pl.when((hop < full) | ((hop == full) & (t % 2 == d)))
            def _(d=d):
                ring_copy(d, hop + 1, t).start()

            @pl.when((hop < far) | (d == 0))
            def _(d=d):
                if d == 0:

                    @pl.when(hop == far)
                    def _():
                        ring_copy(0, far, t).wait_recv()

                core_copy(slot_of(d, hop), t).start()

    def project(slot, p):
        @pl.when(p == 0)
        def _():
            for side in range(2):
                pltpu.make_async_copy(
                    weight.at[:, :, pl.ds(0, depth)], wv.at[side, slot],
                    weight_sem.at[side, slot],
                ).wait()

        core_copy(slot, 2 * p).wait_recv()
        core_copy(slot, 2 * p + 1).wait_recv()
        x = jnp.concatenate(
            [blocks[side, slot, pl.ds(2 * p, 2)].reshape(2 * size, depth) for side in range(2)],
            axis=1,
        )
        w = jnp.concatenate(
            [wv[side, slot].reshape(3 * width, depth) for side in range(2)], axis=1
        )
        acc[p] += nt_dot(w, x)

    def finalize(done):
        for stream in range(3):
            cols = slice(stream * width, (stream + 1) * width)
            start = pl.multiple_of((done - 1) * size + HALO, HALO)
            proj[stream, pl.ds(start, 2 * size), :] = (
                acc[done // 2, cols, :].astype(BF16).T.astype(F32)
            )

        @pl.when((seq == 0) & (done == CHUNKS - 1))
        def _():
            halo_copy().start()

        for t in (done - 1, done):

            @pl.when((seq == 0) | (t > 0))
            def _(t=t):
                gate(t)

            @pl.when(seq == 0)
            def _(t=t):
                gated_copy(t).start()

    def filter_spectra():
        fwd_copy.wait()
        inv_copy.wait()
        lag_copy.wait()
        taps_copy.wait()
        gain_copy.wait()

        @pl.when(seq == 1)
        def _():
            filter_copy().wait_recv()

        def transform(m, carry):
            spec[m] = nt_dot(fwd[...], lags[m])
            return carry

        lax.fori_loop(0, 1 + seq, transform, 0)

        @pl.when(seq == 1)
        def _():
            sign = 1.0 - 2.0 * (
                lax.broadcasted_iota(jnp.int32, (2 * rows, width), 0) % 2
            ).astype(F32)
            spec[1] += sign * spec[0]

    def send_own(t, carry):
        own_copy(t).wait()
        for d in range(2):
            ring_copy(d, 1, t).start()
        core_copy(0, t).start()
        return carry

    lax.fori_loop(0, CHUNKS, send_own, 0)

    for hop in range(far + 1):
        for slot in slots_at(hop):
            for side in range(2):
                weight_copy(side, slot).start()
    lag_copy.start()
    fwd_copy.start()
    inv_copy.start()
    taps_copy.start()
    gain_copy.start()

    @pl.when(seq == 0)
    def _():
        filter_copy().start()

    acc[...] = jnp.zeros_like(acc)

    def stage(n, carry):
        hop, p = 1 + n // 2, n % 2
        pass_on(hop, 2 * p)
        pass_on(hop, 2 * p + 1)

        def one(j, carry):
            project(jnp.minimum(hop - 1 + j * full, last_slot), p)
            return carry

        lax.fori_loop(0, 1 + (hop > 1).astype(jnp.int32) + (hop == far).astype(jnp.int32), one, 0)

        @pl.when(n == 4)
        def _():
            filter_spectra()

        @pl.when(hop == far)
        def _():
            finalize(2 * p + 1)

        return carry

    lax.fori_loop(0, 2 * far, stage, 0)

    def finish(t, carry):
        for hop in range(1, far):
            for d in range(2):
                ring_copy(d, hop, t).wait_send()
        for d in range(2):

            @pl.when(t % 2 == d)
            def _(d=d):
                ring_copy(d, far, t).wait_send()

        for slot in range(last_slot + 1):
            core_copy(slot, t).wait_send()

        return carry

    lax.fori_loop(0, CHUNKS, finish, 0)

    @pl.when(seq == 1)
    def _():
        halo_copy().wait_recv()
        gate(0)

    first = lax.broadcasted_iota(jnp.int32, (rows, width), 0) == 0

    total[...] = jnp.zeros_like(total)

    def term(lag, carry):
        @pl.when(lag == 1)
        def _():
            for t in range(CHUNKS):
                gated_copy(t).wait_recv()

        signal = jnp.dot(fwd[...], gated[lag], preferred_element_type=F32)
        real_part, imag_part = times(
            spec[lag, :rows], spec[lag, rows:], signal[:rows], signal[rows:], first
        )
        total[0] += real_part
        total[1] += imag_part
        return carry

    lax.fori_loop(0, 1 + seq, term, 0)

    scale = jnp.where(first, 0.5, 1.0) / rows
    spectrum = jnp.concatenate(
        [(total[0] * scale).astype(BF16), (total[1] * scale).astype(BF16)], axis=0
    )
    conv = jnp.dot(inv[...], spectrum, preferred_element_type=F32)
    for t in range(CHUNKS):
        here = slice(t * size, (t + 1) * size)
        out[here, :] = (
            short(0, t) * (conv[here] + gain[...] * gated[0, here, :].astype(F32))
        ).astype(BF16)

    @pl.when(seq == 0)
    def _():
        for t in range(CHUNKS):
            gated_copy(t).wait_send()
        halo_copy().wait_send()
        filter_copy().wait_send()


def fused(chips, activations, in_weight, short_taps, long_filter, skip_gain):
    rows, depth = activations.shape
    width = in_weight.shape[1]
    forward, inverse = half_tables(rows)
    size = rows // CHUNKS
    here = pl.BlockSpec(memory_space=pltpu.VMEM)
    there = pl.BlockSpec(memory_space=pltpu.HBM)
    dma = pltpu.SemaphoreType.DMA
    return pl.pallas_call(
        functools.partial(fused_kernel, chips),
        out_shape=pltpu.VMEM((rows, width), BF16),
        in_specs=[there] * 7,
        out_specs=here,
        scratch_shapes=[
            pltpu.VMEM((2, chips, CHUNKS, size, depth), BF16),
            pltpu.VMEM((2, chips, 3, width, depth), BF16),
            pltpu.VMEM((CHUNKS // 2, 3 * width, 2 * size), F32),
            pltpu.VMEM((3, rows + HALO, width), F32),
            pltpu.VMEM((2, rows, width), BF16),
            pltpu.VMEM((2, width, rows), BF16),
            pltpu.VMEM((2 * rows, rows), BF16),
            pltpu.VMEM((rows, 2 * rows), BF16),
            pltpu.VMEM((3, 3, width), F32),
            pltpu.VMEM((1, width), F32),
            pltpu.VMEM((2, 2 * rows, width), F32),
            pltpu.VMEM((2, rows, width), F32),
            dma((chips, CHUNKS)),
            dma((chips, CHUNKS)),
            dma((chips, CHUNKS)),
            dma((chips, CHUNKS)),
            dma((CHUNKS,)),
            dma((2, chips)),
            dma((5,)),
            dma((CHUNKS + 2,)),
            dma((CHUNKS + 2,)),
        ],
        compiler_params=pltpu.CompilerParams(
            collective_id=0, has_side_effects=True, vmem_limit_bytes=63 * 1024 * 1024
        ),
        cost_estimate=pl.CostEstimate(
            flops=2 * rows * chips * 2 * depth * 3 * width,
            bytes_accessed=in_weight.size * 2,
            transcendentals=0,
        ),
    )(
        activations, in_weight, short_taps, long_filter, skip_gain[None, :],
        jnp.asarray(forward), jnp.asarray(inverse),
    )


def general(activations, in_weight, short_taps, long_filter, skip_gain):
    rows = activations.shape[0]
    channels = in_weight.shape[1]
    proj = jnp.einsum(
        "tk,sck->tsc",
        lax.all_gather(activations, "chan", axis=1, tiled=True),
        in_weight,
        preferred_element_type=F32,
    ).astype(BF16)
    earlier = from_behind(proj[rows - 2 :], "seq", 1)
    padded = jnp.concatenate([earlier, proj], axis=0).astype(F32)
    feat = (
        short_taps[:, 0, :] * padded[2:]
        + short_taps[:, 1, :] * padded[1:-1]
        + short_taps[:, 2, :] * padded[:-2]
    )
    gated = (feat[:, 1, :] * feat[:, 2, :]).astype(BF16)
    forward, inverse = (jnp.asarray(table) for table in half_tables(rows))
    seq_count = lax.axis_size("seq")
    all_lags = lax.all_gather(long_filter, "seq", axis=1, tiled=True)
    lag_blocks = all_lags.reshape(channels, seq_count, rows)
    spec = jnp.einsum("ft,cmt->mfc", forward, lag_blocks, preferred_element_type=F32)
    sign = (1.0 - 2.0 * (jnp.arange(2 * rows) % 2)).astype(F32)[:, None]
    spec = spec.at[1:].add(sign * spec[:-1])
    first = jnp.arange(rows)[:, None] == 0
    total = (jnp.zeros((rows, channels), F32), jnp.zeros((rows, channels), F32))
    moving = gated
    for section in range(seq_count):
        if section > 0:
            moving = from_behind(moving, "seq", 1)
        signal = jnp.dot(forward, moving, preferred_element_type=F32)
        part = times(
            spec[section, :rows], spec[section, rows:], signal[:rows], signal[rows:], first
        )
        total = (total[0] + part[0], total[1] + part[1])
    scale = jnp.where(first, 0.5, 1.0) / rows
    spectrum = jnp.concatenate([total[0] * scale, total[1] * scale], axis=0).astype(BF16)
    conv = jnp.dot(inverse, spectrum, preferred_element_type=F32)
    return (feat[:, 0, :] * (conv + skip_gain * gated.astype(F32))).astype(BF16)


def solution(mesh):
    in_specs = (
        P("seq", "chan"),
        P(None, "chan", None),
        P(None, None, "chan"),
        P("chan", "seq"),
        P("chan"),
    )
    out_specs = P("seq", "chan")
    chan = mesh.shape["chan"]
    if mesh.shape["seq"] == 2 and chan == 16:
        on_device = functools.partial(fused, chan // 2)
    else:
        on_device = general
    return jax.shard_map(
        on_device, mesh=mesh, in_specs=in_specs, out_specs=out_specs, check_vma=False
    )
```

```python
import functools
import math

import jax
import jax.numpy as jnp
import ml_dtypes
import numpy as np
from jax import lax
from jax.experimental import pallas as pl
from jax.experimental.pallas import tpu as pltpu
from jax.sharding import PartitionSpec as P

MESH = pl.DeviceIdType.MESH
F32 = jnp.float32
BF16 = jnp.bfloat16
CHUNKS = 4
HALO = 8


def from_behind(block, axis, distance):
    devices = range(lax.axis_size(axis))
    route = [(i - distance, i) for i in devices if i - distance in devices]
    return lax.ppermute(block, axis, route)


def half_tables(length):
    double = 2 * length
    index = np.arange(length, dtype=np.int64)
    phase = ((index[:, None] * index[None, :]) % double).astype(np.float32) * np.float32(
        2.0 * math.pi / double
    )
    cosine = np.cos(phase)
    sine = -np.sin(phase)
    sine[0] = 1.0 - 2.0 * (index % 2)
    forward = np.concatenate([cosine, sine], axis=0).astype(ml_dtypes.bfloat16)
    inverse = np.concatenate([cosine, sine.T], axis=1).astype(ml_dtypes.bfloat16)
    return forward, inverse


def times(fil_real, fil_imag, sig_real, sig_imag, first):
    cross = jnp.where(first, 0.0, fil_imag)
    real_part = fil_real * sig_real - cross * sig_imag
    imag_part = jnp.where(first, fil_imag, fil_real) * sig_imag + cross * sig_real
    return real_part, imag_part


def nt_dot(a, b):
    return lax.dot_general(a, b, (((1,), (1,)), ((), ())), preferred_element_type=F32)


def fused_kernel(
    chips, act, weight, taps_in, filt, gain_in, fwd_in, inv_in, out,
    blocks, wv, acc, proj, gated, lags, fwd, inv, taps, gain, spec, total,
    ring_send, ring_recv, core_send, core_recv, own_sem, weight_sem, load_sem,
    seq_send, seq_recv,
):
    rows, depth = act.shape
    width = taps_in.shape[-1]
    size = rows // CHUNKS
    far = chips // 2
    full = far - 1
    last_slot = 2 * full + 1

    seq = lax.axis_index("seq")
    chan = lax.axis_index("chan")
    chip, core = chan // 2, chan % 2

    def chip_at(place):
        place = lax.rem(place + 2 * chips, chips)
        return jnp.where(place < far, 2 * place, 2 * (chips - 1 - place) + 1)

    place = jnp.where(chip % 2 == 0, chip // 2, chips - 1 - chip // 2)
    ahead = (chip_at(place + 1) * 2 + core, chip_at(place - 1) * 2 + core)
    sibling = chip * 2 + 1 - core

    def slot_of(d, hop):
        if isinstance(hop, int):
            if hop == 0:
                return 0
            return last_slot if hop == far else d * full + hop
        return jnp.where(hop == 0, 0, jnp.where(hop == far, last_slot, d * full + hop))

    def chunk(t):
        return pl.ds(pl.multiple_of(t * size, size), size)

    def ring_copy(d, hop, t):
        src = blocks.at[0, slot_of(d, hop - 1), t]
        slot = slot_of(d, hop)
        return pltpu.make_async_remote_copy(
            src_ref=src, dst_ref=blocks.at[0, slot, t],
            send_sem=ring_send.at[slot, t], recv_sem=ring_recv.at[slot, t],
            device_id=(seq, ahead[d]), device_id_type=MESH,
        )

    def core_copy(slot, t):
        src = blocks.at[0, slot, t]
        return pltpu.make_async_remote_copy(
            src_ref=src, dst_ref=blocks.at[1, slot, t],
            send_sem=core_send.at[slot, t], recv_sem=core_recv.at[slot, t],
            device_id=(seq, sibling), device_id_type=MESH,
        )

    def seq_copy(src, dst, n):
        return pltpu.make_async_remote_copy(
            src_ref=src, dst_ref=dst, send_sem=seq_send.at[n], recv_sem=seq_recv.at[n],
            device_id=(1 - seq, chan), device_id_type=MESH,
        )

    def gated_copy(t):
        return seq_copy(gated.at[0, chunk(t)], gated.at[1, chunk(t)], t)

    def halo_copy():
        return seq_copy(proj.at[:, pl.ds(rows, HALO)], proj.at[:, pl.ds(0, HALO)], CHUNKS)

    def filter_copy():
        return seq_copy(filt, lags.at[0], CHUNKS + 1)

    def own_copy(t):
        return pltpu.make_async_copy(act.at[chunk(t)], blocks.at[0, 0, t], own_sem.at[t])

    def load_weights(hop, ways=2):
        for d in range(ways):
            slot = slot_of(d, hop)
            origin = chip_at(place - hop if d == 0 else place + hop)
            for side in range(2):
                block = origin * 2 + (core if side == 0 else 1 - core)
                cols = pl.ds(pl.multiple_of(block * depth, depth), depth)
                pltpu.make_async_copy(
                    weight.at[:, :, cols], wv.at[side, slot], weight_sem.at[side, slot]
                ).start()

    fwd_copy = pltpu.make_async_copy(fwd_in, fwd, load_sem.at[0])
    inv_copy = pltpu.make_async_copy(inv_in, inv, load_sem.at[1])
    lag_copy = pltpu.make_async_copy(filt, lags.at[seq], load_sem.at[2])
    taps_copy = pltpu.make_async_copy(taps_in, taps, load_sem.at[3])
    gain_copy = pltpu.make_async_copy(gain_in, gain, load_sem.at[4])

    for t in range(CHUNKS):
        own_copy(t).start()
    barrier = pltpu.get_barrier_semaphore()
    for target in ((seq, ahead[0]), (seq, ahead[1]), (seq, sibling), (1 - seq, chan)):
        pl.semaphore_signal(barrier, inc=1, device_id=target, device_id_type=MESH)
    pl.semaphore_wait(barrier, 4)

    @pl.when(seq == 0)
    def _():
        proj[:, pl.ds(0, HALO), :] = jnp.zeros((3, HALO, width), F32)

    def short(stream, t):
        window = proj[stream, pl.ds(pl.multiple_of(t * size, size), size + HALO), :]
        return (
            taps[stream, 0, :][None] * window[HALO:]
            + taps[stream, 1, :][None] * window[HALO - 1 : HALO - 1 + size]
            + taps[stream, 2, :][None] * window[HALO - 2 : HALO - 2 + size]
        )

    def gate(t):
        gated[0, chunk(t), :] = (short(1, t) * short(2, t)).astype(BF16)

    def pass_on(hop, t):
        for d in range(2):

            @pl.when(hop < far)
            def _(d=d):
                ring_copy(d, hop, t).wait_recv()

            @pl.when((hop < full) | ((hop == full) & (t % 2 == d)))
            def _(d=d):
                ring_copy(d, hop + 1, t).start()

            @pl.when((hop < far) | (d == 0))
            def _(d=d):
                if d == 0:

                    @pl.when(hop == far)
                    def _():
                        ring_copy(0, far, t).wait_recv()

                core_copy(slot_of(d, hop), t).start()

    def project(slot, p):
        @pl.when(p == 0)
        def _():
            for side in range(2):
                pltpu.make_async_copy(
                    weight.at[:, :, pl.ds(0, depth)], wv.at[side, slot],
                    weight_sem.at[side, slot],
                ).wait()

        core_copy(slot, 2 * p).wait_recv()
        core_copy(slot, 2 * p + 1).wait_recv()
        x = jnp.concatenate(
            [blocks[side, slot, pl.ds(2 * p, 2)].reshape(2 * size, depth) for side in range(2)],
            axis=1,
        )
        w = jnp.concatenate(
            [wv[side, slot].reshape(3 * width, depth) for side in range(2)], axis=1
        )
        acc[p] += nt_dot(w, x)

    def finalize(done):
        for stream in range(3):
            cols = slice(stream * width, (stream + 1) * width)
            start = pl.multiple_of((done - 1) * size + HALO, HALO)
            proj[stream, pl.ds(start, 2 * size), :] = (
                acc[done // 2, cols, :].astype(BF16).T.astype(F32)
            )

        @pl.when((seq == 0) & (done == CHUNKS - 1))
        def _():
            halo_copy().start()

        for t in (done - 1, done):

            @pl.when((seq == 0) | (t > 0))
            def _(t=t):
                gate(t)

            @pl.when(seq == 0)
            def _(t=t):
                gated_copy(t).start()

    def filter_spectra():
        fwd_copy.wait()
        inv_copy.wait()
        lag_copy.wait()
        taps_copy.wait()
        gain_copy.wait()

        @pl.when(seq == 1)
        def _():
            filter_copy().wait_recv()

        def transform(m, carry):
            spec[m] = nt_dot(fwd[...], lags[m])
            return carry

        lax.fori_loop(0, 1 + seq, transform, 0)

        @pl.when(seq == 1)
        def _():
            sign = 1.0 - 2.0 * (
                lax.broadcasted_iota(jnp.int32, (2 * rows, width), 0) % 2
            ).astype(F32)
            spec[1] += sign * spec[0]

    def send_own(t, carry):
        own_copy(t).wait()
        for d in range(2):
            ring_copy(d, 1, t).start()
        core_copy(0, t).start()
        return carry

    lax.fori_loop(0, CHUNKS, send_own, 0)

    load_weights(0, 1)
    load_weights(1)

    @pl.when(seq == 0)
    def _():
        filter_copy().start()

    acc[...] = jnp.zeros_like(acc)

    def stage(n, carry):
        hop, p = 1 + n // 2, n % 2

        @pl.when((p == 0) & (hop < full))
        def _():
            load_weights(hop + 1)

        @pl.when((p == 0) & (hop == full))
        def _():
            load_weights(far, 1)

        @pl.when(n == 1)
        def _():
            for load in (lag_copy, fwd_copy, inv_copy, taps_copy, gain_copy):
                load.start()

        def one(j, carry):
            @pl.when((j == 2) | ((j == 0) & (hop < far)))
            def _():
                pass_on(hop, 2 * p)
                pass_on(hop, 2 * p + 1)

            project(jnp.minimum(hop - 1 + j * full, last_slot), p)
            return carry

        lax.fori_loop(0, 1 + (hop > 1).astype(jnp.int32) + (hop == far).astype(jnp.int32), one, 0)

        @pl.when(n == 4)
        def _():
            filter_spectra()

        @pl.when(hop == far)
        def _():
            finalize(2 * p + 1)

        return carry

    lax.fori_loop(0, 2 * far, stage, 0)

    def finish(t, carry):
        for hop in range(1, far):
            for d in range(2):
                ring_copy(d, hop, t).wait_send()
        for d in range(2):

            @pl.when(t % 2 == d)
            def _(d=d):
                ring_copy(d, far, t).wait_send()

        for slot in range(last_slot + 1):
            core_copy(slot, t).wait_send()

        return carry

    lax.fori_loop(0, CHUNKS, finish, 0)

    @pl.when(seq == 1)
    def _():
        halo_copy().wait_recv()
        gate(0)

    first = lax.broadcasted_iota(jnp.int32, (rows, width), 0) == 0

    total[...] = jnp.zeros_like(total)

    def term(lag, carry):
        @pl.when(lag == 1)
        def _():
            for t in range(CHUNKS):
                gated_copy(t).wait_recv()

        signal = jnp.dot(fwd[...], gated[lag], preferred_element_type=F32)
        real_part, imag_part = times(
            spec[lag, :rows], spec[lag, rows:], signal[:rows], signal[rows:], first
        )
        total[0] += real_part
        total[1] += imag_part
        return carry

    lax.fori_loop(0, 1 + seq, term, 0)

    scale = jnp.where(first, 0.5, 1.0) / rows
    spectrum = jnp.concatenate(
        [(total[0] * scale).astype(BF16), (total[1] * scale).astype(BF16)], axis=0
    )
    conv = jnp.dot(inv[...], spectrum, preferred_element_type=F32)
    for t in range(CHUNKS):
        here = slice(t * size, (t + 1) * size)
        out[here, :] = (
            short(0, t) * (conv[here] + gain[...] * gated[0, here, :].astype(F32))
        ).astype(BF16)

    @pl.when(seq == 0)
    def _():
        for t in range(CHUNKS):
            gated_copy(t).wait_send()
        halo_copy().wait_send()
        filter_copy().wait_send()


def fused(chips, activations, in_weight, short_taps, long_filter, skip_gain):
    rows, depth = activations.shape
    width = in_weight.shape[1]
    forward, inverse = half_tables(rows)
    size = rows // CHUNKS
    here = pl.BlockSpec(memory_space=pltpu.VMEM)
    there = pl.BlockSpec(memory_space=pltpu.HBM)
    dma = pltpu.SemaphoreType.DMA
    return pl.pallas_call(
        functools.partial(fused_kernel, chips),
        out_shape=pltpu.VMEM((rows, width), BF16),
        in_specs=[there] * 7,
        out_specs=here,
        scratch_shapes=[
            pltpu.VMEM((2, chips, CHUNKS, size, depth), BF16),
            pltpu.VMEM((2, chips, 3, width, depth), BF16),
            pltpu.VMEM((CHUNKS // 2, 3 * width, 2 * size), F32),
            pltpu.VMEM((3, rows + HALO, width), F32),
            pltpu.VMEM((2, rows, width), BF16),
            pltpu.VMEM((2, width, rows), BF16),
            pltpu.VMEM((2 * rows, rows), BF16),
            pltpu.VMEM((rows, 2 * rows), BF16),
            pltpu.VMEM((3, 3, width), F32),
            pltpu.VMEM((1, width), F32),
            pltpu.VMEM((2, 2 * rows, width), F32),
            pltpu.VMEM((2, rows, width), F32),
            dma((chips, CHUNKS)),
            dma((chips, CHUNKS)),
            dma((chips, CHUNKS)),
            dma((chips, CHUNKS)),
            dma((CHUNKS,)),
            dma((2, chips)),
            dma((5,)),
            dma((CHUNKS + 2,)),
            dma((CHUNKS + 2,)),
        ],
        compiler_params=pltpu.CompilerParams(
            collective_id=0, has_side_effects=True, vmem_limit_bytes=63 * 1024 * 1024
        ),
        cost_estimate=pl.CostEstimate(
            flops=2 * rows * chips * 2 * depth * 3 * width,
            bytes_accessed=in_weight.size * 2,
            transcendentals=0,
        ),
    )(
        activations, in_weight, short_taps, long_filter, skip_gain[None, :],
        jnp.asarray(forward), jnp.asarray(inverse),
    )


def general(activations, in_weight, short_taps, long_filter, skip_gain):
    rows = activations.shape[0]
    channels = in_weight.shape[1]
    proj = jnp.einsum(
        "tk,sck->tsc",
        lax.all_gather(activations, "chan", axis=1, tiled=True),
        in_weight,
        preferred_element_type=F32,
    ).astype(BF16)
    earlier = from_behind(proj[rows - 2 :], "seq", 1)
    padded = jnp.concatenate([earlier, proj], axis=0).astype(F32)
    feat = (
        short_taps[:, 0, :] * padded[2:]
        + short_taps[:, 1, :] * padded[1:-1]
        + short_taps[:, 2, :] * padded[:-2]
    )
    gated = (feat[:, 1, :] * feat[:, 2, :]).astype(BF16)
    forward, inverse = (jnp.asarray(table) for table in half_tables(rows))
    seq_count = lax.axis_size("seq")
    all_lags = lax.all_gather(long_filter, "seq", axis=1, tiled=True)
    lag_blocks = all_lags.reshape(channels, seq_count, rows)
    spec = jnp.einsum("ft,cmt->mfc", forward, lag_blocks, preferred_element_type=F32)
    sign = (1.0 - 2.0 * (jnp.arange(2 * rows) % 2)).astype(F32)[:, None]
    spec = spec.at[1:].add(sign * spec[:-1])
    first = jnp.arange(rows)[:, None] == 0
    total = (jnp.zeros((rows, channels), F32), jnp.zeros((rows, channels), F32))
    moving = gated
    for section in range(seq_count):
        if section > 0:
            moving = from_behind(moving, "seq", 1)
        signal = jnp.dot(forward, moving, preferred_element_type=F32)
        part = times(
            spec[section, :rows], spec[section, rows:], signal[:rows], signal[rows:], first
        )
        total = (total[0] + part[0], total[1] + part[1])
    scale = jnp.where(first, 0.5, 1.0) / rows
    spectrum = jnp.concatenate([total[0] * scale, total[1] * scale], axis=0).astype(BF16)
    conv = jnp.dot(inverse, spectrum, preferred_element_type=F32)
    return (feat[:, 0, :] * (conv + skip_gain * gated.astype(F32))).astype(BF16)


def solution(mesh):
    in_specs = (
        P("seq", "chan"),
        P(None, "chan", None),
        P(None, None, "chan"),
        P("chan", "seq"),
        P("chan"),
    )
    out_specs = P("seq", "chan")
    chan = mesh.shape["chan"]
    if mesh.shape["seq"] == 2 and chan == 16:
        on_device = functools.partial(fused, chan // 2)
    else:
        on_device = general
    return jax.shard_map(
        on_device, mesh=mesh, in_specs=in_specs, out_specs=out_specs, check_vma=False
    )
```

```python
import functools
import math

import jax
import jax.numpy as jnp
import ml_dtypes
import numpy as np
from jax import lax
from jax.experimental import pallas as pl
from jax.experimental.pallas import tpu as pltpu
from jax.sharding import PartitionSpec as P

MESH = pl.DeviceIdType.MESH
F32 = jnp.float32
BF16 = jnp.bfloat16
CHUNKS = 4
HALO = 8


def from_behind(block, axis, distance):
    devices = range(lax.axis_size(axis))
    route = [(i - distance, i) for i in devices if i - distance in devices]
    return lax.ppermute(block, axis, route)


def half_tables(length):
    double = 2 * length
    index = np.arange(length, dtype=np.int64)
    phase = ((index[:, None] * index[None, :]) % double).astype(np.float32) * np.float32(
        2.0 * math.pi / double
    )
    cosine = np.cos(phase)
    sine = -np.sin(phase)
    sine[0] = 1.0 - 2.0 * (index % 2)
    forward = np.concatenate([cosine, sine], axis=0).astype(ml_dtypes.bfloat16)
    inverse = np.concatenate([cosine, sine.T], axis=1).astype(ml_dtypes.bfloat16)
    return forward, inverse


def times(fil_real, fil_imag, sig_real, sig_imag, first):
    cross = jnp.where(first, 0.0, fil_imag)
    real_part = fil_real * sig_real - cross * sig_imag
    imag_part = jnp.where(first, fil_imag, fil_real) * sig_imag + cross * sig_real
    return real_part, imag_part


def nt_dot(a, b):
    return lax.dot_general(a, b, (((1,), (1,)), ((), ())), preferred_element_type=F32)


def fused_kernel(
    chips, act, weight, taps_in, filt, gain_in, fwd_in, inv_in, out,
    blocks, wv, acc, proj, gated, lags, fwd, inv, taps, gain, spec, total,
    ring_send, ring_recv, core_send, core_recv, own_sem, weight_sem, load_sem,
    seq_send, seq_recv,
):
    rows, depth = act.shape
    width = taps_in.shape[-1]
    size = rows // CHUNKS
    far = chips // 2
    full = far - 1
    last_slot = 2 * full + 1

    seq = lax.axis_index("seq")
    chan = lax.axis_index("chan")
    chip, core = chan // 2, chan % 2

    def chip_at(place):
        place = lax.rem(place + 2 * chips, chips)
        return jnp.where(place < far, 2 * place, 2 * (chips - 1 - place) + 1)

    place = jnp.where(chip % 2 == 0, chip // 2, chips - 1 - chip // 2)
    ahead = (chip_at(place + 1) * 2 + core, chip_at(place - 1) * 2 + core)
    sibling = chip * 2 + 1 - core

    def slot_of(d, hop):
        if isinstance(hop, int):
            if hop == 0:
                return 0
            return last_slot if hop == far else d * full + hop
        return jnp.where(hop == 0, 0, jnp.where(hop == far, last_slot, d * full + hop))

    def chunk(t):
        return pl.ds(pl.multiple_of(t * size, size), size)

    def ring_copy(d, hop, t):
        src = blocks.at[0, slot_of(d, hop - 1), t]
        slot = slot_of(d, hop)
        return pltpu.make_async_remote_copy(
            src_ref=src, dst_ref=blocks.at[0, slot, t],
            send_sem=ring_send.at[slot, t], recv_sem=ring_recv.at[slot, t],
            device_id=(seq, ahead[d]), device_id_type=MESH,
        )

    def core_copy(slot, t):
        src = blocks.at[0, slot, t]
        return pltpu.make_async_remote_copy(
            src_ref=src, dst_ref=blocks.at[1, slot, t],
            send_sem=core_send.at[slot, t], recv_sem=core_recv.at[slot, t],
            device_id=(seq, sibling), device_id_type=MESH,
        )

    def seq_copy(src, dst, n):
        return pltpu.make_async_remote_copy(
            src_ref=src, dst_ref=dst, send_sem=seq_send.at[n], recv_sem=seq_recv.at[n],
            device_id=(1 - seq, chan), device_id_type=MESH,
        )

    def gated_copy(t):
        return seq_copy(gated.at[0, chunk(t)], gated.at[1, chunk(t)], t)

    def halo_copy():
        return seq_copy(proj.at[:, pl.ds(rows, HALO)], proj.at[:, pl.ds(0, HALO)], CHUNKS)

    def filter_copy():
        return seq_copy(filt, lags.at[0], CHUNKS + 1)

    def own_copy(t):
        return pltpu.make_async_copy(act.at[chunk(t)], blocks.at[0, 0, t], own_sem.at[t])

    def load_weights(hop, ways=2):
        for d in range(ways):
            slot = slot_of(d, hop)
            origin = chip_at(place - hop if d == 0 else place + hop)
            for side in range(2):
                block = origin * 2 + (core if side == 0 else 1 - core)
                cols = pl.ds(pl.multiple_of(block * depth, depth), depth)
                pltpu.make_async_copy(
                    weight.at[:, :, cols], wv.at[side, slot], weight_sem.at[side, slot]
                ).start()

    fwd_copy = pltpu.make_async_copy(fwd_in, fwd, load_sem.at[0])
    inv_copy = pltpu.make_async_copy(inv_in, inv, load_sem.at[1])
    lag_copy = pltpu.make_async_copy(filt, lags.at[seq], load_sem.at[2])
    taps_copy = pltpu.make_async_copy(taps_in, taps, load_sem.at[3])
    gain_copy = pltpu.make_async_copy(gain_in, gain, load_sem.at[4])

    for t in range(CHUNKS):
        own_copy(t).start()
    barrier = pltpu.get_barrier_semaphore()
    for target in ((seq, ahead[0]), (seq, ahead[1]), (seq, sibling), (1 - seq, chan)):
        pl.semaphore_signal(barrier, inc=1, device_id=target, device_id_type=MESH)
    pl.semaphore_wait(barrier, 4)

    @pl.when(seq == 0)
    def _():
        proj[:, pl.ds(0, HALO), :] = jnp.zeros((3, HALO, width), F32)

    def short(stream, t):
        window = proj[stream, pl.ds(pl.multiple_of(t * size, size), size + HALO), :]
        return (
            taps[stream, 0, :][None] * window[HALO:]
            + taps[stream, 1, :][None] * window[HALO - 1 : HALO - 1 + size]
            + taps[stream, 2, :][None] * window[HALO - 2 : HALO - 2 + size]
        )

    def gate(t):
        gated[0, chunk(t), :] = (short(1, t) * short(2, t)).astype(BF16)

    def pass_on(hop, t):
        for d in range(2):

            @pl.when(hop < far)
            def _(d=d):
                ring_copy(d, hop, t).wait_recv()

            @pl.when((hop < full) | ((hop == full) & (t % 2 == d)))
            def _(d=d):
                ring_copy(d, hop + 1, t).start()

            @pl.when((hop < far) | (d == 0))
            def _(d=d):
                if d == 0:

                    @pl.when(hop == far)
                    def _():
                        ring_copy(0, far, t).wait_recv()

                core_copy(slot_of(d, hop), t).start()

    def project(slot, p):
        @pl.when(p == 0)
        def _():
            for side in range(2):
                pltpu.make_async_copy(
                    weight.at[:, :, pl.ds(0, depth)], wv.at[side, slot],
                    weight_sem.at[side, slot],
                ).wait()

        core_copy(slot, 2 * p).wait_recv()
        core_copy(slot, 2 * p + 1).wait_recv()
        x = jnp.concatenate(
            [blocks[side, slot, pl.ds(2 * p, 2)].reshape(2 * size, depth) for side in range(2)],
            axis=1,
        )
        w = jnp.concatenate(
            [wv[side, slot].reshape(3 * width, depth) for side in range(2)], axis=1
        )
        acc[p] += nt_dot(w, x)

    def finalize(done):
        for stream in range(3):
            cols = slice(stream * width, (stream + 1) * width)
            start = pl.multiple_of((done - 1) * size + HALO, HALO)
            proj[stream, pl.ds(start, 2 * size), :] = (
                acc[done // 2, cols, :].astype(BF16).T.astype(F32)
            )

        @pl.when((seq == 0) & (done == CHUNKS - 1))
        def _():
            halo_copy().start()

        for t in (done - 1, done):

            @pl.when((seq == 0) | (t > 0))
            def _(t=t):
                gate(t)

            @pl.when(seq == 0)
            def _(t=t):
                gated_copy(t).start()

    def filter_spectra():
        fwd_copy.wait()
        inv_copy.wait()
        lag_copy.wait()
        taps_copy.wait()
        gain_copy.wait()

        @pl.when(seq == 1)
        def _():
            filter_copy().wait_recv()

        def transform(m, carry):
            spec[m] = nt_dot(fwd[...], lags[m])
            return carry

        lax.fori_loop(0, 1 + seq, transform, 0)

        @pl.when(seq == 1)
        def _():
            sign = 1.0 - 2.0 * (
                lax.broadcasted_iota(jnp.int32, (2 * rows, width), 0) % 2
            ).astype(F32)
            spec[1] += sign * spec[0]

    def send_own(t, carry):
        own_copy(t).wait()
        for d in range(2):
            ring_copy(d, 1, t).start()
        core_copy(0, t).start()
        return carry

    lax.fori_loop(0, CHUNKS, send_own, 0)

    load_weights(0, 1)
    load_weights(1)

    acc[...] = jnp.zeros_like(acc)

    def stage(n, carry):
        hop, p = 1 + n // 2, n % 2

        @pl.when((p == 0) & (hop < full))
        def _():
            load_weights(hop + 1)

        @pl.when((p == 0) & (hop == full))
        def _():
            load_weights(far, 1)

        @pl.when(n == 1)
        def _():
            for load in (lag_copy, fwd_copy, inv_copy, taps_copy, gain_copy):
                load.start()

            @pl.when(seq == 0)
            def _():
                filter_copy().start()

        def one(j, carry):
            @pl.when((j == 2) | ((j == 0) & (hop < far)))
            def _():
                pass_on(hop, 2 * p)
                pass_on(hop, 2 * p + 1)

            project(jnp.minimum(hop - 1 + j * full, last_slot), p)
            return carry

        lax.fori_loop(0, 1 + (hop > 1).astype(jnp.int32) + (hop == far).astype(jnp.int32), one, 0)

        @pl.when(n == 4)
        def _():
            filter_spectra()

        @pl.when(hop == far)
        def _():
            finalize(2 * p + 1)

        return carry

    lax.fori_loop(0, 2 * far, stage, 0)

    def finish(t, carry):
        for hop in range(1, far):
            for d in range(2):
                ring_copy(d, hop, t).wait_send()
        for d in range(2):

            @pl.when(t % 2 == d)
            def _(d=d):
                ring_copy(d, far, t).wait_send()

        for slot in range(last_slot + 1):
            core_copy(slot, t).wait_send()

        return carry

    lax.fori_loop(0, CHUNKS, finish, 0)

    @pl.when(seq == 1)
    def _():
        halo_copy().wait_recv()
        gate(0)

    first = lax.broadcasted_iota(jnp.int32, (rows, width), 0) == 0

    total[...] = jnp.zeros_like(total)

    def term(lag, carry):
        @pl.when(lag == 1)
        def _():
            for t in range(CHUNKS):
                gated_copy(t).wait_recv()

        signal = jnp.dot(fwd[...], gated[lag], preferred_element_type=F32)
        real_part, imag_part = times(
            spec[lag, :rows], spec[lag, rows:], signal[:rows], signal[rows:], first
        )
        total[0] += real_part
        total[1] += imag_part
        return carry

    lax.fori_loop(0, 1 + seq, term, 0)

    scale = jnp.where(first, 0.5, 1.0) / rows
    spectrum = jnp.concatenate(
        [(total[0] * scale).astype(BF16), (total[1] * scale).astype(BF16)], axis=0
    )
    conv = jnp.dot(inv[...], spectrum, preferred_element_type=F32)
    for t in range(CHUNKS):
        here = slice(t * size, (t + 1) * size)
        out[here, :] = (
            short(0, t) * (conv[here] + gain[...] * gated[0, here, :].astype(F32))
        ).astype(BF16)

    @pl.when(seq == 0)
    def _():
        for t in range(CHUNKS):
            gated_copy(t).wait_send()
        halo_copy().wait_send()
        filter_copy().wait_send()


def fused(chips, activations, in_weight, short_taps, long_filter, skip_gain):
    rows, depth = activations.shape
    width = in_weight.shape[1]
    forward, inverse = half_tables(rows)
    size = rows // CHUNKS
    here = pl.BlockSpec(memory_space=pltpu.VMEM)
    there = pl.BlockSpec(memory_space=pltpu.HBM)
    dma = pltpu.SemaphoreType.DMA
    return pl.pallas_call(
        functools.partial(fused_kernel, chips),
        out_shape=pltpu.VMEM((rows, width), BF16),
        in_specs=[there] * 7,
        out_specs=here,
        scratch_shapes=[
            pltpu.VMEM((2, chips, CHUNKS, size, depth), BF16),
            pltpu.VMEM((2, chips, 3, width, depth), BF16),
            pltpu.VMEM((CHUNKS // 2, 3 * width, 2 * size), F32),
            pltpu.VMEM((3, rows + HALO, width), F32),
            pltpu.VMEM((2, rows, width), BF16),
            pltpu.VMEM((2, width, rows), BF16),
            pltpu.VMEM((2 * rows, rows), BF16),
            pltpu.VMEM((rows, 2 * rows), BF16),
            pltpu.VMEM((3, 3, width), F32),
            pltpu.VMEM((1, width), F32),
            pltpu.VMEM((2, 2 * rows, width), F32),
            pltpu.VMEM((2, rows, width), F32),
            dma((chips, CHUNKS)),
            dma((chips, CHUNKS)),
            dma((chips, CHUNKS)),
            dma((chips, CHUNKS)),
            dma((CHUNKS,)),
            dma((2, chips)),
            dma((5,)),
            dma((CHUNKS + 2,)),
            dma((CHUNKS + 2,)),
        ],
        compiler_params=pltpu.CompilerParams(
            collective_id=0, has_side_effects=True, vmem_limit_bytes=63 * 1024 * 1024
        ),
        cost_estimate=pl.CostEstimate(
            flops=2 * rows * chips * 2 * depth * 3 * width,
            bytes_accessed=in_weight.size * 2,
            transcendentals=0,
        ),
    )(
        activations, in_weight, short_taps, long_filter, skip_gain[None, :],
        jnp.asarray(forward), jnp.asarray(inverse),
    )


def general(activations, in_weight, short_taps, long_filter, skip_gain):
    rows = activations.shape[0]
    channels = in_weight.shape[1]
    proj = jnp.einsum(
        "tk,sck->tsc",
        lax.all_gather(activations, "chan", axis=1, tiled=True),
        in_weight,
        preferred_element_type=F32,
    ).astype(BF16)
    earlier = from_behind(proj[rows - 2 :], "seq", 1)
    padded = jnp.concatenate([earlier, proj], axis=0).astype(F32)
    feat = (
        short_taps[:, 0, :] * padded[2:]
        + short_taps[:, 1, :] * padded[1:-1]
        + short_taps[:, 2, :] * padded[:-2]
    )
    gated = (feat[:, 1, :] * feat[:, 2, :]).astype(BF16)
    forward, inverse = (jnp.asarray(table) for table in half_tables(rows))
    seq_count = lax.axis_size("seq")
    all_lags = lax.all_gather(long_filter, "seq", axis=1, tiled=True)
    lag_blocks = all_lags.reshape(channels, seq_count, rows)
    spec = jnp.einsum("ft,cmt->mfc", forward, lag_blocks, preferred_element_type=F32)
    sign = (1.0 - 2.0 * (jnp.arange(2 * rows) % 2)).astype(F32)[:, None]
    spec = spec.at[1:].add(sign * spec[:-1])
    first = jnp.arange(rows)[:, None] == 0
    total = (jnp.zeros((rows, channels), F32), jnp.zeros((rows, channels), F32))
    moving = gated
    for section in range(seq_count):
        if section > 0:
            moving = from_behind(moving, "seq", 1)
        signal = jnp.dot(forward, moving, preferred_element_type=F32)
        part = times(
            spec[section, :rows], spec[section, rows:], signal[:rows], signal[rows:], first
        )
        total = (total[0] + part[0], total[1] + part[1])
    scale = jnp.where(first, 0.5, 1.0) / rows
    spectrum = jnp.concatenate([total[0] * scale, total[1] * scale], axis=0).astype(BF16)
    conv = jnp.dot(inverse, spectrum, preferred_element_type=F32)
    return (feat[:, 0, :] * (conv + skip_gain * gated.astype(F32))).astype(BF16)


def solution(mesh):
    in_specs = (
        P("seq", "chan"),
        P(None, "chan", None),
        P(None, None, "chan"),
        P("chan", "seq"),
        P("chan"),
    )
    out_specs = P("seq", "chan")
    chan = mesh.shape["chan"]
    if mesh.shape["seq"] == 2 and chan == 16:
        on_device = functools.partial(fused, chan // 2)
    else:
        on_device = general
    return jax.shard_map(
        on_device, mesh=mesh, in_specs=in_specs, out_specs=out_specs, check_vma=False
    )
```
